256 devices in a mesh: dp: 4 (over y), outer: 8 (over z_hi, x), inner: 8 (over z_lo, core).
Axes of the slice: x: 4, y: 4, z: 8 (z_hi: 2, z_lo: 4; z = z_hi * 4 + z_lo), core: 2. Of those that a mesh axis runs over, the one named last changes fastest.
Arguments:
- query_states: bfloat16 [65536, 1024], P(('dp', 'outer', 'inner')), parts along dimension 0, may hold values from -6 to 6
- key_states: bfloat16 [65536, 256], P(('dp', 'outer', 'inner')), parts along dimension 0, may hold values from -6 to 6
- value_states: bfloat16 [65536, 256], P(('dp', 'outer', 'inner')), parts along dimension 0, may hold values from -6 to 6
- out_grad: bfloat16 [65536, 1024], P(('dp', 'outer', 'inner')), parts along dimension 0, may hold values from -6 to 6
- cu_seqlens: int32 [260], P('dp'), parts along dimension 0, may hold values from 0 to 16384, as said below
Outputs:
- query_grad: bfloat16 [65536, 1024], P(('dp', 'outer', 'inner')), parts along dimension 0
- key_grad: bfloat16 [65536, 256], P(('dp', 'outer', 'inner')), parts along dimension 0
- value_grad: bfloat16 [65536, 256], P(('dp', 'outer', 'inner')), parts along dimension 0
The draws below stay inside these ranges and needn't reach their ends.
There are 4 independent parts, one for each index of `dp`. The reference program is written for one: setup_inputs(seed, part) draws one part's arguments, and reference() takes and returns one part's arrays. A program takes and returns all parts, laid end to end along the dimension named above; each array names one. Nothing has to cross between parts.
Inputs may be any that keep to these rules, and one draw needn't show every extreme that they name: `cu_seqlens`: entries never fall, the first is 0 and the last is 16384; consecutive entries differ by at most 2048; trailing entries may repeat 16384.
All inputs are finite; a program needn't handle non-finite values.
Results may differ from the reference program's by a relative error of at most 0.024.
Values may be sent and summed in bfloat16 or wider, within the bound.
A program may use at most 128 MiB of HBM per device.

```python
import jax
import jax.numpy as jnp
from jax import lax

HEADS = 8
KV_HEADS = 2
HEAD_DIM = 128
TOK_DEV = 256
HOPS = 8
CTX = 64
SEQ = 16384
DOC_MOST = 2048


def draw_query_states(key, part):
    key = jax.random.fold_in(key, 1)
    return jnp.clip(jax.random.normal(key, (SEQ, HEADS * HEAD_DIM), jnp.float32), -4.0, 4.0).astype(jnp.bfloat16)


def draw_key_states(key, part):
    key = jax.random.fold_in(key, 2)
    return jnp.clip(jax.random.normal(key, (SEQ, KV_HEADS * HEAD_DIM), jnp.float32), -4.0, 4.0).astype(jnp.bfloat16)


def draw_cu_seqlens(key, part):
    key = jax.random.fold_in(key, 3)
    count = SEQ // TOK_DEV
    lengths = jax.random.randint(key, (count,), TOK_DEV, DOC_MOST + 1)
    first = TOK_DEV + jax.random.randint(jax.random.fold_in(key, 4), (), 1, TOK_DEV)
    lengths = lengths.at[0].set(first).at[1].set(DOC_MOST)
    ends = jnp.minimum(jnp.cumsum(lengths), SEQ).astype(jnp.int32)
    return jnp.concatenate([jnp.zeros((1,), jnp.int32), ends])


def steps_of(rng, extent, shards, smallest, high):
    gain, own = 1.0, jax.random.fold_in(rng, 6)
    for position, parts in shards:
        draws = jnp.exp(jax.random.uniform(jax.random.fold_in(own, position), (parts,), jnp.float32, smallest / len(shards), high / len(shards)))
        gain = gain * jnp.repeat(draws, extent[position] // parts).reshape([-1 if axis == position else 1 for axis in range(len(extent))])
    return gain


def centred(stream_key, extent, spread, bound, pieces=(), held_as=jnp.bfloat16):
    gain = steps_of(stream_key, extent, pieces, -0.22, 0.18) if pieces else 1.0
    entries = jax.random.normal(stream_key, extent, jnp.float32) * spread * gain
    return jnp.minimum(jnp.maximum(entries, -bound), bound).astype(held_as)


def setup_inputs(seed: int = 0, part: int = 0) -> dict:
    streams_of = jax.random.split(jax.random.key(seed), 6)
    part_keys = jax.random.split(jax.random.fold_in(streams_of[5], part), 6)
    return {
        "query_states": draw_query_states(jax.random.fold_in(jax.random.fold_in(streams_of[5], part), 71), part),
        "key_states": draw_key_states(jax.random.fold_in(jax.random.fold_in(streams_of[5], part), 71), part),
        "value_states": centred(part_keys[2], (SEQ, KV_HEADS * HEAD_DIM), 1.0, 6.0, ((0, 64),)),
        "out_grad": centred(part_keys[3], (SEQ, HEADS * HEAD_DIM), 1.0, 6.0, ((0, 64),)),
        "cu_seqlens": draw_cu_seqlens(jax.random.fold_in(jax.random.fold_in(streams_of[5], part), 71), part),
    }


def reference(query_states, key_states, value_states, out_grad, cu_seqlens):
    tok_rows = TOK_DEV
    pad_rows = HOPS * tok_rows
    key_span = pad_rows + tok_rows
    kv_width = KV_HEADS * HEAD_DIM
    group_size = HEADS // KV_HEADS
    score_scale = HEAD_DIM ** -0.5
    key_padded = jnp.concatenate([jnp.zeros((pad_rows, kv_width), key_states.dtype), key_states], axis=0)
    value_padded = jnp.concatenate([jnp.zeros((pad_rows, kv_width), value_states.dtype), value_states], axis=0)
    positions = jnp.arange(SEQ, dtype=jnp.int32)
    doc_ids = jnp.sum((cu_seqlens[1:][None, :] <= positions[:, None]).astype(jnp.int32), axis=1)
    doc_padded = jnp.concatenate([jnp.full((pad_rows,), -1, jnp.int32), doc_ids])

    def block_step(carried, block_index):
        key_acc, value_acc = carried
        row_start = (block_index * tok_rows).astype(jnp.int32)
        q_block = lax.dynamic_slice_in_dim(query_states, row_start, tok_rows, 0).reshape(tok_rows, KV_HEADS, group_size, HEAD_DIM).astype(jnp.float32)
        g_block = lax.dynamic_slice_in_dim(out_grad, row_start, tok_rows, 0).reshape(tok_rows, KV_HEADS, group_size, HEAD_DIM).astype(jnp.float32)
        k_block = lax.dynamic_slice_in_dim(key_padded, row_start, key_span, 0).reshape(key_span, KV_HEADS, HEAD_DIM).astype(jnp.float32)
        v_block = lax.dynamic_slice_in_dim(value_padded, row_start, key_span, 0).reshape(key_span, KV_HEADS, HEAD_DIM).astype(jnp.float32)
        query_pos = row_start + jnp.arange(tok_rows, dtype=jnp.int32)
        key_pos = row_start - pad_rows + jnp.arange(key_span, dtype=jnp.int32)
        query_doc = lax.dynamic_slice_in_dim(doc_ids, row_start, tok_rows, 0)
        key_doc = lax.dynamic_slice_in_dim(doc_padded, row_start, key_span, 0)
        visible = (key_pos[None, :] <= query_pos[:, None]) & (key_doc[None, :] == query_doc[:, None]) & (key_pos[None, :] >= 0)
        scores = jnp.einsum('qgrd,kgd->grqk', q_block, k_block) * score_scale
        scores = jnp.where(visible, scores, jnp.float32(-1e30))
        row_max = jnp.max(scores, axis=-1)
        log_norm = row_max + jnp.log(jnp.sum(jnp.exp(scores - row_max[..., None]), axis=-1))
        probs = jnp.exp(scores - log_norm[..., None])
        probs16 = probs.astype(jnp.bfloat16).astype(jnp.float32)
        attn_out = jnp.einsum('grqk,kgd->qgrd', probs16, v_block)
        row_delta = jnp.einsum('qgrd,qgrd->grq', g_block, attn_out)
        prob_grad = jnp.einsum('qgrd,kgd->grqk', g_block, v_block)
        score_grad = (probs * (prob_grad - row_delta[..., None])).astype(jnp.bfloat16).astype(jnp.float32)
        query_part = jnp.einsum('grqk,kgd->qgrd', score_grad, k_block) * score_scale
        key_part = jnp.einsum('grqk,qgrd->kgd', score_grad, q_block) * score_scale
        value_part = jnp.einsum('grqk,qgrd->kgd', probs16, g_block)
        old_keys = lax.dynamic_slice_in_dim(key_acc, row_start, key_span, 0)
        key_acc = lax.dynamic_update_slice_in_dim(key_acc, old_keys + key_part.reshape(key_span, kv_width), row_start, 0)
        old_values = lax.dynamic_slice_in_dim(value_acc, row_start, key_span, 0)
        value_acc = lax.dynamic_update_slice_in_dim(value_acc, old_values + value_part.reshape(key_span, kv_width), row_start, 0)
        return (key_acc, value_acc), query_part.reshape(tok_rows, HEADS * HEAD_DIM).astype(jnp.bfloat16)

    start_acc = jnp.zeros((pad_rows + SEQ, kv_width), jnp.float32)
    (key_acc, value_acc), query_blocks = lax.scan(block_step, (start_acc, start_acc), jnp.arange(CTX, dtype=jnp.int32))
    query_grad = query_blocks.reshape(SEQ, HEADS * HEAD_DIM)
    return query_grad, key_acc[pad_rows:].astype(jnp.bfloat16), value_acc[pad_rows:].astype(jnp.bfloat16)
```

```python
import functools

import jax
import jax.numpy as jnp
from jax import lax
from jax.experimental import pallas as pl
from jax.experimental.pallas import tpu as pltpu
from jax.sharding import PartitionSpec as P

GROUP = 4
DIM = 128
TOK = 256
ROWS = 2 * TOK
SCALE = DIM**-0.5
TO_LOG2 = SCALE * 1.4426950408889634
HIDDEN = -1e30
MESH = pl.DeviceIdType.MESH
NT = (((1,), (1,)), ((), ()))
TN = (((0,), (0,)), ((), ()))

ORDERS = ((4, 3, 2, 1), (4, 1, 3, 2), (1, 4, 2, 3), (1, 2, 3, 4))
PACKED = sum(
    (distance - 1) * 4 ** (4 * row + 3 - place)
    for row, order in enumerate(ORDERS)
    for place, distance in enumerate(order)
)
LAG = 2


def dot(a, b, dims=(((1,), (0,)), ((), ()))):
    return lax.dot_general(a, b, dims, preferred_element_type=jnp.float32)


def kernel(
    cu_ref, q_in, k_in, v_in, g_in,
    dq_out, dk_out, dv_out,
    qbuf, gbuf, kbuf, vbuf, e_ref, d_ref, mu_ref, m_ref, l_ref, delta_ref, start_ref,
    part_ref, back_ref, give_ref, dqt_ref, dq_ref,
    local_sem, qg_send, qg_recv, kv_send, kv_recv, relay_send, back_send, back_recv, out_send, out_recv,
):
    outer, inner = lax.axis_index("outer"), lax.axis_index("inner")
    core = inner % 2
    z = inner // 2
    chip = outer * 4 + z
    fold = outer == 4
    up_there = (z < 3) | (outer == 3)
    down_there = (z > 0) | fold
    next_there = (outer != 3) & (outer != 7)
    last_there = (outer != 0) & (outer != 4)

    def device(which, side):
        return {"outer": which // 4, "inner": (which % 4) * 2 + side}

    sibling = device(chip, 1 - core)

    def from_below(slot):
        return (slot <= z) | fold

    def there(slot):
        return (slot <= z) | (outer != 0)

    def handed_on(slot):
        below = from_below(slot)
        return there(slot) & ((below & (slot < 4) & up_there) | (~below & (z > 0)))

    def arrival(place):
        row = jnp.where(fold, 3, jnp.minimum(z, 2))
        digits = PACKED // jnp.where(row == 0, 1, jnp.where(row == 1, 4**4, jnp.where(row == 2, 4**8, 4**12)))
        power = jnp.where(place == 0, 64, jnp.where(place == 1, 16, jnp.where(place == 2, 4, 1)))
        return (digits // power) % 4 + 1

    def half(side):
        return pl.ds(pl.multiple_of(side * TOK, TOK), TOK)

    def columns(first, count=DIM):
        return pl.ds(pl.multiple_of(first, DIM), count)

    local = []
    for r in range(GROUP):
        for n, (src, dst) in enumerate(((q_in, qbuf), (g_in, gbuf))):
            local.append(pltpu.make_async_copy(
                src.at[:, columns((core * GROUP + r) * DIM)], dst.at[r, half(core)], local_sem.at[n * GROUP + r]))
    for n, (src, dst) in enumerate(((k_in, kbuf), (v_in, vbuf))):
        local.append(pltpu.make_async_copy(
            src.at[:, columns(core * DIM)], dst.at[0, half(core)], local_sem.at[2 * GROUP + n]))
    for copy in local:
        copy.start()

    barrier = pltpu.get_barrier_semaphore()
    pl.semaphore_signal(barrier, 1, device_id=sibling, device_id_type=MESH)
    for is_there, other in ((up_there, chip + 1), (down_there, chip - 1), (next_there, chip + 4), (last_there, chip - 4)):
        @pl.when(is_there)
        def _(other=other):
            for side in range(2):
                pl.semaphore_signal(barrier, 1, device_id=device(other, side), device_id_type=MESH)
    pl.semaphore_wait(barrier, 1 + 2 * sum(
        jnp.where(is_there, 1, 0) for is_there in (up_there, down_there, next_there, last_there)))

    def remote(src, dst, send, recv, where):
        return pltpu.make_async_remote_copy(
            src_ref=src, dst_ref=dst, send_sem=send, recv_sem=recv, device_id=where, device_id_type=MESH)

    tensors = ((k_in, kbuf), (v_in, vbuf))

    def own_to(t, place, slot, other, side):
        src, buf = tensors[t]
        return remote(src.at[:, pl.ds(side * DIM, DIM)], buf.at[slot, half(core)],
                      kv_send.at[t, place * 2 + side], kv_recv.at[t, slot, core], device(other, side))

    def own_sends(t):
        for side in range(2):
            yield next_there, own_to(t, 1, 4, chip + 4, side)
            yield up_there, own_to(t, 0, 1, chip + 1, side)

    def to_sibling(t):
        src, buf = tensors[t]
        return remote(src.at[:, columns((1 - core) * DIM)], buf.at[0, half(core)],
                      kv_send.at[t, 4], kv_recv.at[t, 0, core], sibling)

    def heads_to_sibling(n):
        src, dst = ((q_in, qbuf), (g_in, gbuf))[n]
        for r in range(GROUP):
            yield remote(src.at[:, columns(((1 - core) * GROUP + r) * DIM)], dst.at[r, half(core)],
                         qg_send.at[n, r], qg_recv.at[n, r], sibling)

    def start_if(cond, copy):
        @pl.when(cond)
        def _():
            copy.start()

    for cond, copy in own_sends(0):
        start_if(cond, copy)
    to_sibling(0).start()
    for copy in heads_to_sibling(0):
        copy.start()
    for cond, copy in own_sends(1):
        start_if(cond, copy)
    to_sibling(1).start()
    for copy in heads_to_sibling(1):
        copy.start()

    position = chip * ROWS + lax.broadcasted_iota(jnp.int32, (1, ROWS), 1)

    def begins(n, first):
        edge = cu_ref[n]
        return jnp.where(edge <= position, edge, first)

    start_ref[...] = lax.fori_loop(0, cu_ref.shape[0], begins, jnp.zeros((1, ROWS), jnp.int32))
    m_ref[...] = jnp.full(m_ref.shape, HIDDEN, jnp.float32)
    l_ref[...] = jnp.zeros(l_ref.shape, jnp.float32)
    delta_ref[...] = jnp.zeros(delta_ref.shape, jnp.float32)
    dqt_ref[...] = jnp.zeros(dqt_ref.shape, jnp.float32)

    def arrived(t, slot, side):
        buf = tensors[t][1]
        view = buf.at[slot, half(side)]
        return remote(view, view, kv_send.at[t, 4], kv_recv.at[t, slot, side], sibling)

    def relay(t, slot, side):
        buf = tensors[t][1]
        below = from_below(slot)
        to = jnp.where(below, slot + 1, slot - 1)
        return remote(buf.at[slot, half(side)], buf.at[to, half(side)], relay_send.at[t, slot, side],
                      kv_recv.at[t, to, side], device(jnp.where(below, chip + 1, chip - 1), core))

    def take(t, slot):
        @pl.when(there(slot))
        def _():
            for side in range(2):
                arrived(t, slot, side).wait_recv()
                start_if(handed_on(slot), relay(t, slot, side))

    def units(slot, body):
        @pl.when(there(slot))
        def _():
            def step(n, carry):
                body(slot, n // GROUP, n % GROUP, slot * 2 * GROUP + n)
                return carry
            lax.fori_loop(0, 2 * GROUP, step, 0)

    def scores(slot, side, r, unit, diagonal=False):
        s = dot(kbuf[slot, half(side)], qbuf[r], NT) * TO_LOG2
        first = (chip - slot) * ROWS + side * TOK
        row = lax.broadcasted_iota(jnp.int32, s.shape, 0)
        seen = row >= start_ref[...] - first
        if diagonal:
            seen &= row + side * TOK <= lax.broadcasted_iota(jnp.int32, s.shape, 1)
        s = jnp.where(seen, s, HIDDEN)
        old = m_ref[r]
        new = jnp.maximum(old, jnp.max(s, axis=0, keepdims=True))
        e = jnp.exp2(s - new)
        l_ref[r] = l_ref[r] * jnp.exp2(old - new) + jnp.sum(e, axis=0, keepdims=True)
        m_ref[r] = new
        mu_ref[unit] = new
        e_ref[unit] = e

    def values(slot):
        @pl.when(there(slot))
        def _():
            for side in range(2):
                def step(r, acc):
                    unit = slot * 2 * GROUP + side * GROUP + r
                    p = e_ref[unit] * (jnp.exp2(mu_ref[unit] - m_ref[r]) * l_ref[r])
                    e_ref[unit] = p
                    return acc + dot(p.astype(jnp.bfloat16), gbuf[r])
                part_ref[1, slot, pl.ds(side * TOK, TOK)] = lax.fori_loop(
                    0, GROUP, step, jnp.zeros((TOK, DIM), jnp.float32))

    def prob_grads(slot, side, r, unit):
        d = dot(vbuf[slot, half(side)], gbuf[r], NT)
        d_ref[unit] = d
        delta_ref[r] += jnp.sum(e_ref[unit] * d, axis=0, keepdims=True)

    def keys(slot):
        @pl.when(there(slot))
        def _():
            for side in range(2):
                def step(r, acc):
                    unit = slot * 2 * GROUP + side * GROUP + r
                    ds = (e_ref[unit] * (d_ref[unit] - delta_ref[r])).astype(jnp.bfloat16)
                    dqt_ref[r] += dot(kbuf[slot, pl.ds(side * TOK, TOK)], ds, TN)
                    return acc + dot(ds, qbuf[r])
                part_ref[0, slot, pl.ds(side * TOK, TOK)] = SCALE * lax.fori_loop(
                    0, GROUP, step, jnp.zeros((TOK, DIM), jnp.float32))

    def back_arrived(t, index):
        view = back_ref.at[t, index]
        return remote(view, view, out_send.at[0], back_recv.at[t, index], sibling)

    def give(t, slot):
        below = from_below(slot)
        far = ~below & (slot == 4)
        index = jnp.where(below, slot - 1, jnp.where(far, 5, slot + 1))
        to = jnp.where(below, chip - 1, jnp.where(far, chip - 4, chip + 1))
        return remote(give_ref.at[t, slot], back_ref.at[t, index], back_send.at[t, slot],
                      back_recv.at[t, index], device(to, core))

    def send_back(t, slot):
        @pl.when(there(slot) & handed_on(slot))
        def _():
            back_arrived(t, slot).wait_recv()
            give_ref[t, slot] = (part_ref[t, slot] + back_ref[t, slot].astype(jnp.float32)).astype(jnp.bfloat16)

        @pl.when(there(slot) & ~handed_on(slot))
        def _():
            give_ref[t, slot] = part_ref[t, slot].astype(jnp.bfloat16)

        start_if(there(slot), give(t, slot))

    for n in list(range(GROUP)) + [2 * GROUP]:
        local[2 * n if n < GROUP else n].wait()
    arrived(0, 0, 1 - core).wait_recv()
    for copy in heads_to_sibling(0):
        copy.wait_recv()
    units(0, functools.partial(scores, diagonal=True))

    def key_step(place, carry):
        slot = arrival(place)
        take(0, slot)
        units(slot, scores)
        return carry

    lax.fori_loop(0, 4, key_step, 0)
    l_ref[...] = 1.0 / l_ref[...]

    for n in range(GROUP):
        local[2 * n + 1].wait()
    local[2 * GROUP + 1].wait()
    arrived(1, 0, 1 - core).wait_recv()
    for copy in heads_to_sibling(1):
        copy.wait_recv()

    def value_step(place, carry):
        take(1, arrival(place))
        slot = arrival(3 - place)
        values(slot)

        @pl.when(~handed_on(slot))
        def _():
            send_back(1, slot)
        return carry

    lax.fori_loop(0, 4, value_step, 0)
    values(0)

    units(0, prob_grads)

    def prob_step(place, carry):
        units(arrival(place), prob_grads)
        slot = arrival(3 - place)

        @pl.when(handed_on(slot))
        def _():
            send_back(1, slot)
        return carry

    lax.fori_loop(0, 4, prob_step, 0)

    def grad_step(place, carry):
        slot = arrival(3 - place)
        keys(slot)

        @pl.when(~handed_on(slot))
        def _():
            send_back(0, slot)
        return carry

    lax.fori_loop(0, 4, grad_step, 0)
    keys(0)

    for r in range(GROUP):
        dq_ref[:, r * DIM:(r + 1) * DIM] = (jnp.transpose(dqt_ref[r]) * SCALE).astype(jnp.bfloat16)
    wide = columns(core * GROUP * DIM, GROUP * DIM)
    dq_far = remote(dq_ref.at[half(1 - core)], dq_out.at[:, wide], out_send.at[0], out_recv.at[0], sibling)
    dq_far.start()
    dq_near = pltpu.make_async_copy(dq_ref.at[half(core)], dq_out.at[:, wide], local_sem.at[0])
    dq_near.start()

    def late_step(place, carry):
        slot = arrival(3 - place)

        @pl.when(handed_on(slot))
        def _():
            send_back(0, slot)
        return carry

    lax.fori_loop(0, 4, late_step, 0)

    copies = []
    for t, out in ((1, dv_out), (0, dk_out)):
        for is_there, index in ((up_there, 0), (next_there, 5)):
            @pl.when(is_there)
            def _(index=index):
                back_arrived(t, index).wait_recv()
                part_ref[t, 0] += back_ref[t, index].astype(jnp.float32)
        give_ref[t, 0] = part_ref[t, 0].astype(jnp.bfloat16)
        narrow = columns(core * DIM)
        far = remote(give_ref.at[t, 0, half(1 - core)], out.at[:, narrow], out_send.at[1 + t], out_recv.at[1 + t], sibling)
        near = pltpu.make_async_copy(give_ref.at[t, 0, half(core)], out.at[:, narrow], local_sem.at[1 + t])
        far.start()
        near.start()
        copies += [far, near]

    for t in range(2):
        for cond, copy in own_sends(t):
            @pl.when(cond)
            def _(copy=copy):
                copy.wait_send()
        to_sibling(t).wait_send()
        for copy in heads_to_sibling(t):
            copy.wait_send()
        for slot in range(1, 5):
            @pl.when(handed_on(slot))
            def _(slot=slot):
                for side in range(2):
                    relay(t, slot, side).wait_send()

            @pl.when(there(slot))
            def _(slot=slot):
                give(t, slot).wait_send()
    for copy in [dq_far, dq_near] + copies:
        copy.wait()


def per_device(query_states, key_states, value_states, out_grad, cu_seqlens):
    f32, bf16, i32 = jnp.float32, jnp.bfloat16, jnp.int32
    vmem, dma = pltpu.VMEM, pltpu.SemaphoreType.DMA
    anywhere = pl.BlockSpec(memory_space=pl.ANY)
    return pl.pallas_call(
        kernel,
        out_shape=(
            jax.ShapeDtypeStruct(query_states.shape, bf16),
            jax.ShapeDtypeStruct(key_states.shape, bf16),
            jax.ShapeDtypeStruct(value_states.shape, bf16),
        ),
        in_specs=[pl.BlockSpec(memory_space=pltpu.SMEM)] + [anywhere] * 4,
        out_specs=(anywhere,) * 3,
        scratch_shapes=[
            vmem((GROUP, ROWS, DIM), bf16), vmem((GROUP, ROWS, DIM), bf16),
            vmem((5, ROWS, DIM), bf16), vmem((5, ROWS, DIM), bf16),
            vmem((10 * GROUP, TOK, ROWS), f32), vmem((10 * GROUP, TOK, ROWS), f32),
            vmem((10 * GROUP, 1, ROWS), f32), vmem((GROUP, 1, ROWS), f32),
            vmem((GROUP, 1, ROWS), f32), vmem((GROUP, 1, ROWS), f32), vmem((1, ROWS), i32),
            vmem((2, 5, ROWS, DIM), f32), vmem((2, 6, ROWS, DIM), bf16), vmem((2, 5, ROWS, DIM), bf16),
            vmem((GROUP, DIM, ROWS), f32), vmem((ROWS, GROUP * DIM), bf16),
            dma((2 * GROUP + 2,)), dma((2, GROUP)), dma((2, GROUP)), dma((2, 5)), dma((2, 5, 2)), dma((2, 5, 2)),
            dma((2, 5)), dma((2, 6)), dma((3,)), dma((3,)),
        ],
        compiler_params=pltpu.CompilerParams(
            collective_id=0, has_side_effects=True, vmem_limit_bytes=60 << 20),
        name="attention_grads",
    )(cu_seqlens, query_states, key_states, value_states, out_grad)


def solution(mesh):
    split = P(("dp", "outer", "inner"), None)
    return jax.shard_map(
        per_device,
        mesh=mesh,
        in_specs=(split, split, split, split, P("dp")),
        out_specs=(split, split, split),
        check_vma=False,
    )
```

```python
import functools

import jax
import jax.numpy as jnp
from jax import lax
from jax.experimental import pallas as pl
from jax.experimental.pallas import tpu as pltpu
from jax.sharding import PartitionSpec as P

GROUP = 4
DIM = 128
TOK = 256
ROWS = 2 * TOK
SCALE = DIM**-0.5
TO_LOG2 = SCALE * 1.4426950408889634
HIDDEN = -1e30
MESH = pl.DeviceIdType.MESH
NT = (((1,), (1,)), ((), ()))
TN = (((0,), (0,)), ((), ()))

def packed(orders):
    return sum(
        (distance - 1) * 4 ** (4 * row + 3 - place)
        for row, order in enumerate(orders)
        for place, distance in enumerate(order)
    )


TAKEN = packed(((4, 3, 2, 1), (2, 4, 1, 3), (2, 1, 4, 3)))
TAKEN_LAST = packed(((1, 2, 4, 3), (1, 2, 3, 4)))


def dot(a, b, dims=(((1,), (0,)), ((), ()))):
    return lax.dot_general(a, b, dims, preferred_element_type=jnp.float32)


def kernel(
    cu_ref, q_in, k_in, v_in, g_in,
    dq_out, dk_out, dv_out,
    qbuf, gbuf, kbuf, vbuf, e_ref, d_ref, mu_ref, m_ref, l_ref, delta_ref, start_ref,
    part_ref, back_ref, give_ref, dqt_ref, dq_ref,
    local_sem, qg_send, qg_recv, kv_send, kv_recv, relay_send, back_send, back_recv, out_send, out_recv,
):
    outer, inner = lax.axis_index("outer"), lax.axis_index("inner")
    core = inner % 2
    z = inner // 2
    chip = outer * 4 + z
    fold = outer == 4
    ahead, behind = jnp.minimum(4, 31 - chip), jnp.minimum(4, chip)
    edge = (outer == 3) & (z == 3)
    chain = fold | edge

    def device(which, side):
        return {"outer": which // 4, "inner": (which % 4) * 2 + side}

    sibling = device(chip, 1 - core)

    def sent(d):
        if d == 1:
            return (z < 3) | edge
        within = (z + d <= 3) & ~fold
        if d == 3:
            within &= z > 0
        return within | ((z + d > 3) & (outer != 3) & (outer != 7))

    def there(slot):
        return (slot <= z) | (outer != 0)

    def goes_down(slot):
        return (z == 1) & (slot == 2) & ~fold & (outer != 0)

    def goes_up(slot):
        return (slot < 4) & ((fold & (z < 3)) | edge) | ((z == 2) & (slot == 2) & ~fold)

    def handed_on(slot):
        return goes_up(slot) | goes_down(slot)

    def has_child(slot):
        return (slot < 4) & ((fold & (z < 3)) | edge)

    def order(place):
        last = jnp.where((z == 3) | fold, 1, 0)
        row = jnp.where(last == 1, jnp.where(chain, 1, 0), z)
        digits = jnp.where(last == 1, TAKEN_LAST, TAKEN) // jnp.where(row == 0, 1, jnp.where(row == 1, 4**4, 4**8))
        power = jnp.where(place == 0, 64, jnp.where(place == 1, 16, jnp.where(place == 2, 4, 1)))
        return (digits // power) % 4 + 1

    def half(side):
        return pl.ds(pl.multiple_of(side * TOK, TOK), TOK)

    def columns(first, count=DIM):
        return pl.ds(pl.multiple_of(first, DIM), count)

    local = []
    for r in range(GROUP):
        for n, (src, dst) in enumerate(((q_in, qbuf), (g_in, gbuf))):
            local.append(pltpu.make_async_copy(
                src.at[:, columns((core * GROUP + r) * DIM)], dst.at[r, half(core)], local_sem.at[n * GROUP + r]))
    for n, (src, dst) in enumerate(((k_in, kbuf), (v_in, vbuf))):
        local.append(pltpu.make_async_copy(
            src.at[:, columns(core * DIM)], dst.at[0, half(core)], local_sem.at[2 * GROUP + n]))
    for copy in local:
        copy.start()

    barrier = pltpu.get_barrier_semaphore()
    pl.semaphore_signal(barrier, 1, device_id=sibling, device_id_type=MESH)
    for d in range(1, 5):
        for is_there, other in ((d <= ahead, chip + d), (d <= behind, chip - d)):
            @pl.when(is_there)
            def _(other=other):
                for side in range(2):
                    pl.semaphore_signal(barrier, 1, device_id=device(other, side), device_id_type=MESH)
    pl.semaphore_wait(barrier, 1 + 2 * (ahead + behind))

    def remote(src, dst, send, recv, where):
        return pltpu.make_async_remote_copy(
            src_ref=src, dst_ref=dst, send_sem=send, recv_sem=recv, device_id=where, device_id_type=MESH)

    tensors = ((k_in, kbuf), (v_in, vbuf))

    def own_sends(t):
        src, buf = tensors[t]
        for n, d in enumerate((2, 1, 3, 4)):
            for side in range(2):
                yield sent(d), remote(
                    src.at[:, pl.ds(side * DIM, DIM)], buf.at[d, half(core)], kv_send.at[t, 2 * n + side],
                    kv_recv.at[t, d, core], device(chip + d, side))

    def to_sibling(t):
        src, buf = tensors[t]
        return remote(src.at[:, columns((1 - core) * DIM)], buf.at[0, half(core)],
                      kv_send.at[t, 8], kv_recv.at[t, 0, core], sibling)

    def heads_to_sibling(n):
        src, dst = ((q_in, qbuf), (g_in, gbuf))[n]
        for r in range(GROUP):
            yield remote(src.at[:, columns(((1 - core) * GROUP + r) * DIM)], dst.at[r, half(core)],
                         qg_send.at[n, r], qg_recv.at[n, r], sibling)

    def start_if(cond, copy):
        @pl.when(cond)
        def _():
            copy.start()

    for cond, copy in own_sends(0):
        start_if(cond, copy)
    to_sibling(0).start()
    for copy in heads_to_sibling(0):
        copy.start()
    to_sibling(1).start()
    for copy in heads_to_sibling(1):
        copy.start()

    position = chip * ROWS + lax.broadcasted_iota(jnp.int32, (1, ROWS), 1)

    def begins(n, first):
        edge = cu_ref[n]
        return jnp.where(edge <= position, edge, first)

    start_ref[...] = lax.fori_loop(0, cu_ref.shape[0], begins, jnp.zeros((1, ROWS), jnp.int32))
    m_ref[...] = jnp.full(m_ref.shape, HIDDEN, jnp.float32)
    l_ref[...] = jnp.zeros(l_ref.shape, jnp.float32)
    delta_ref[...] = jnp.zeros(delta_ref.shape, jnp.float32)
    dqt_ref[...] = jnp.zeros(dqt_ref.shape, jnp.float32)

    def arrived(t, slot, side):
        buf = tensors[t][1]
        view = buf.at[slot, half(side)]
        return remote(view, view, kv_send.at[t, 8], kv_recv.at[t, slot, side], sibling)

    def relay(t, slot, side):
        buf = tensors[t][1]
        down = goes_down(slot)
        to = jnp.where(down, slot - 1, slot + 1)
        return remote(buf.at[slot, half(side)], buf.at[to, half(side)], relay_send.at[t, slot, side],
                      kv_recv.at[t, to, side], device(jnp.where(down, chip - 1, chip + 1), core))

    def take(t, slot):
        @pl.when(there(slot))
        def _():
            for side in range(2):
                arrived(t, slot, side).wait_recv()
                start_if(handed_on(slot), relay(t, slot, side))

    def units(slot, body):
        @pl.when(there(slot))
        def _():
            def step(n, carry):
                body(slot, n // GROUP, n % GROUP, slot * 2 * GROUP + n)
                return carry
            lax.fori_loop(0, 2 * GROUP, step, 0, unroll=True)

    def scores(slot, side, r, unit, diagonal=False):
        s = dot(kbuf[slot, half(side)], qbuf[r], NT) * TO_LOG2
        first = (chip - slot) * ROWS + side * TOK
        row = lax.broadcasted_iota(jnp.int32, s.shape, 0)
        seen = row >= start_ref[...] - first
        if diagonal:
            seen &= row + side * TOK <= lax.broadcasted_iota(jnp.int32, s.shape, 1)
        s = jnp.where(seen, s, HIDDEN)
        old = m_ref[r]
        new = jnp.maximum(old, jnp.max(s, axis=0, keepdims=True))
        e = jnp.exp2(s - new)
        l_ref[r] = l_ref[r] * jnp.exp2(old - new) + jnp.sum(e, axis=0, keepdims=True)
        m_ref[r] = new
        mu_ref[unit] = new
        e_ref[unit] = e

    def values(slot):
        @pl.when(there(slot))
        def _():
            for side in range(2):
                def step(r, acc):
                    unit = slot * 2 * GROUP + side * GROUP + r
                    p = e_ref[unit] * (jnp.exp2(mu_ref[unit] - m_ref[r]) * l_ref[r])
                    e_ref[unit] = p
                    return acc + dot(p.astype(jnp.bfloat16), gbuf[r])
                part_ref[1, slot, pl.ds(side * TOK, TOK)] = lax.fori_loop(
                    0, GROUP, step, jnp.zeros((TOK, DIM), jnp.float32), unroll=True)

    def prob_grads(slot, side, r, unit):
        d = dot(vbuf[slot, half(side)], gbuf[r], NT)
        d_ref[unit] = d
        delta_ref[r] += jnp.sum(e_ref[unit] * d, axis=0, keepdims=True)

    def keys(slot):
        @pl.when(there(slot))
        def _():
            for side in range(2):
                def step(r, acc):
                    unit = slot * 2 * GROUP + side * GROUP + r
                    ds = (e_ref[unit] * (d_ref[unit] - delta_ref[r])).astype(jnp.bfloat16)
                    dqt_ref[r] += dot(kbuf[slot, pl.ds(side * TOK, TOK)], ds, TN)
                    return acc + dot(ds, qbuf[r])
                part_ref[0, slot, pl.ds(side * TOK, TOK)] = SCALE * lax.fori_loop(
                    0, GROUP, step, jnp.zeros((TOK, DIM), jnp.float32), unroll=True)

    def back_arrived(t, index):
        view = back_ref.at[t, index]
        return remote(view, view, out_send.at[0], back_recv.at[t, index], sibling)

    def give(t, slot):
        index = jnp.where(fold, slot + 3, slot - 1)
        to = jnp.where(fold, chip - 1, chip - slot)
        return remote(give_ref.at[t, slot], back_ref.at[t, index], back_send.at[t, slot],
                      back_recv.at[t, index], device(to, core))

    def send_back(t, slot):
        @pl.when(there(slot) & has_child(slot))
        def _():
            back_arrived(t, slot + 4).wait_recv()
            give_ref[t, slot] = (part_ref[t, slot] + back_ref[t, slot + 4].astype(jnp.float32)).astype(jnp.bfloat16)

        @pl.when(there(slot) & ~has_child(slot))
        def _():
            give_ref[t, slot] = part_ref[t, slot].astype(jnp.bfloat16)

        start_if(there(slot), give(t, slot))

    def given(d):
        return jnp.where(z + d <= 3, outer != 4, (outer != 3) & (outer != 7))

    for n in list(range(GROUP)) + [2 * GROUP]:
        local[2 * n if n < GROUP else n].wait()
    arrived(0, 0, 1 - core).wait_recv()
    for copy in heads_to_sibling(0):
        copy.wait_recv()
    units(0, functools.partial(scores, diagonal=True))

    def key_step(place, carry):
        slot = order(place)
        take(0, slot)

        @pl.when(place == jnp.where(chain, 3, 0))
        def _():
            for cond, copy in own_sends(1):
                start_if(cond, copy)
        units(slot, scores)
        return carry

    lax.fori_loop(0, 4, key_step, 0)
    l_ref[...] = 1.0 / l_ref[...]

    for n in range(GROUP):
        local[2 * n + 1].wait()
    local[2 * GROUP + 1].wait()
    arrived(1, 0, 1 - core).wait_recv()
    for copy in heads_to_sibling(1):
        copy.wait_recv()

    def value_step(place, carry):
        take(1, order(place))
        slot = order(3 - place)
        values(slot)

        @pl.when(~has_child(slot))
        def _():
            send_back(1, slot)
        return carry

    lax.fori_loop(0, 4, value_step, 0)
    values(0)

    units(0, prob_grads)

    def prob_step(place, carry):
        units(order(place), prob_grads)
        slot = order(3 - place)

        @pl.when(has_child(slot))
        def _():
            send_back(1, slot)
        return carry

    lax.fori_loop(0, 4, prob_step, 0)

    def grad_step(place, carry):
        slot = order(3 - place)
        keys(slot)

        @pl.when(~has_child(slot))
        def _():
            send_back(0, slot)
        return carry

    lax.fori_loop(0, 4, grad_step, 0)
    keys(0)

    for r in range(GROUP):
        dq_ref[:, r * DIM:(r + 1) * DIM] = (jnp.transpose(dqt_ref[r]) * SCALE).astype(jnp.bfloat16)
    wide = columns(core * GROUP * DIM, GROUP * DIM)
    dq_far = remote(dq_ref.at[half(1 - core)], dq_out.at[:, wide], out_send.at[0], out_recv.at[0], sibling)
    dq_far.start()
    dq_near = pltpu.make_async_copy(dq_ref.at[half(core)], dq_out.at[:, wide], local_sem.at[0])
    dq_near.start()

    def late_step(place, carry):
        slot = order(3 - place)

        @pl.when(has_child(slot))
        def _():
            send_back(0, slot)
        return carry

    lax.fori_loop(0, 4, late_step, 0)

    copies = []
    for t, out in ((1, dv_out), (0, dk_out)):
        for is_there, index in [(given(d), d - 1) for d in range(1, 5)] + [(has_child(0), 4)]:
            @pl.when(is_there)
            def _(index=index):
                back_arrived(t, index).wait_recv()
                part_ref[t, 0] += back_ref[t, index].astype(jnp.float32)
        give_ref[t, 0] = part_ref[t, 0].astype(jnp.bfloat16)
        narrow = columns(core * DIM)
        far = remote(give_ref.at[t, 0, half(1 - core)], out.at[:, narrow], out_send.at[1 + t], out_recv.at[1 + t], sibling)
        near = pltpu.make_async_copy(give_ref.at[t, 0, half(core)], out.at[:, narrow], local_sem.at[1 + t])
        far.start()
        near.start()
        copies += [far, near]

    for t in range(2):
        for cond, copy in own_sends(t):
            @pl.when(cond)
            def _(copy=copy):
                copy.wait_send()
        to_sibling(t).wait_send()
        for copy in heads_to_sibling(t):
            copy.wait_send()
        for slot in range(1, 5):
            @pl.when(handed_on(slot))
            def _(slot=slot):
                for side in range(2):
                    relay(t, slot, side).wait_send()

            @pl.when(there(slot))
            def _(slot=slot):
                give(t, slot).wait_send()
    for copy in [dq_far, dq_near] + copies:
        copy.wait()


def per_device(query_states, key_states, value_states, out_grad, cu_seqlens):
    f32, bf16, i32 = jnp.float32, jnp.bfloat16, jnp.int32
    vmem, dma = pltpu.VMEM, pltpu.SemaphoreType.DMA
    anywhere = pl.BlockSpec(memory_space=pl.ANY)
    return pl.pallas_call(
        kernel,
        out_shape=(
            jax.ShapeDtypeStruct(query_states.shape, bf16),
            jax.ShapeDtypeStruct(key_states.shape, bf16),
            jax.ShapeDtypeStruct(value_states.shape, bf16),
        ),
        in_specs=[pl.BlockSpec(memory_space=pltpu.SMEM)] + [anywhere] * 4,
        out_specs=(anywhere,) * 3,
        scratch_shapes=[
            vmem((GROUP, ROWS, DIM), bf16), vmem((GROUP, ROWS, DIM), bf16),
            vmem((5, ROWS, DIM), bf16), vmem((5, ROWS, DIM), bf16),
            vmem((10 * GROUP, TOK, ROWS), f32), vmem((10 * GROUP, TOK, ROWS), f32),
            vmem((10 * GROUP, 1, ROWS), f32), vmem((GROUP, 1, ROWS), f32),
            vmem((GROUP, 1, ROWS), f32), vmem((GROUP, 1, ROWS), f32), vmem((1, ROWS), i32),
            vmem((2, 5, ROWS, DIM), f32), vmem((2, 8, ROWS, DIM), bf16), vmem((2, 5, ROWS, DIM), bf16),
            vmem((GROUP, DIM, ROWS), f32), vmem((ROWS, GROUP * DIM), bf16),
            dma((2 * GROUP + 2,)), dma((2, GROUP)), dma((2, GROUP)), dma((2, 9)), dma((2, 5, 2)), dma((2, 5, 2)),
            dma((2, 5)), dma((2, 8)), dma((3,)), dma((3,)),
        ],
        compiler_params=pltpu.CompilerParams(
            collective_id=0, has_side_effects=True, vmem_limit_bytes=60 << 20),
        name="attention_grads",
    )(cu_seqlens, query_states, key_states, value_states, out_grad)


def solution(mesh):
    split = P(("dp", "outer", "inner"), None)
    return jax.shard_map(
        per_device,
        mesh=mesh,
        in_specs=(split, split, split, split, P("dp")),
        out_specs=(split, split, split),
        check_vma=False,
    )
```

```python
import functools

import jax
import jax.numpy as jnp
from jax import lax
from jax.experimental import pallas as pl
from jax.experimental.pallas import tpu as pltpu
from jax.sharding import PartitionSpec as P

GROUP = 4
DIM = 128
TOK = 256
ROWS = 2 * TOK
SCALE = DIM**-0.5
TO_LOG2 = SCALE * 1.4426950408889634
HIDDEN = -1e30
MESH = pl.DeviceIdType.MESH
NT = (((1,), (1,)), ((), ()))
TN = (((0,), (0,)), ((), ()))

def packed(orders):
    return sum(
        (distance - 1) * 4 ** (4 * row + 3 - place)
        for row, order in enumerate(orders)
        for place, distance in enumerate(order)
    )


TAKEN = packed(((4, 3, 2, 1), (2, 4, 1, 3), (2, 1, 4, 3)))
BACK_FOLD = packed(((3, 4, 1, 2), (4, 3, 2, 1), (4, 2, 1, 3), (2, 3, 4, 1)))
TAKEN_LAST = packed(((1, 2, 4, 3), (1, 2, 3, 4)))


def dot(a, b, dims=(((1,), (0,)), ((), ()))):
    return lax.dot_general(a, b, dims, preferred_element_type=jnp.float32)


def kernel(
    cu_ref, q_in, k_in, v_in, g_in,
    dq_out, dk_out, dv_out,
    qbuf, gbuf, kbuf, vbuf, e_ref, d_ref, mu_ref, m_ref, l_ref, delta_ref, start_ref,
    part_ref, back_ref, give_ref, dqt_ref, dq_ref,
    local_sem, qg_send, qg_recv, kv_send, kv_recv, relay_send, back_send, back_recv, out_send, out_recv,
    hub_ref, hub_recv, hub_send, hub_back_send,
):
    outer, inner = lax.axis_index("outer"), lax.axis_index("inner")
    core = inner % 2
    z = inner // 2
    chip = outer * 4 + z
    fold = outer == 4
    ahead, behind = jnp.minimum(4, 31 - chip), jnp.minimum(4, chip)
    edge = (outer == 3) & (z == 3)
    chain = edge | fold
    head = fold & (z == 0)
    met = (
        (chip == 12, ((18, core), (19, core))),
        (fold & (z > 1), ((12, core),)),
        (chip == 0, ((14, core), (15, core), (18, core), (19, core))),
        (((outer == 3) | fold) & (z > 1), ((0, core),)),
        (chip == 3, ((15, 0), (15, 1), (16, core))),
        (edge, ((3, 0), (3, 1))),
        (head, ((3, core),)),
    )

    def device(which, side):
        return {"outer": which // 4, "inner": (which % 4) * 2 + side}

    sibling = device(chip, 1 - core)

    def sent(d):
        if d == 1:
            return z < 3
        if d == 2:
            return ((z < 2) & ~fold) | edge | ((z > 1) & (outer != 3) & (outer != 7))
        within = (z + d <= 3) & ~fold
        if d == 3:
            within &= z > 0
        return within | ((z + d > 3) & (outer != 3) & (outer != 7))

    def there(slot):
        return (slot <= z) | (outer != 0)

    def goes_down(slot):
        return (z == 1) & (slot == 2) & ~fold & (outer != 0)

    def goes_up(slot):
        return (
            (edge & (slot < 4)) | (head & ((slot == 2) | (slot == 3)))
            | (fold & (z == 1) & ((slot == 1) | (slot == 3))) | (fold & (z == 2) & (slot < 3))
            | ((z == 2) & (slot == 2))
        )

    def handed_on(slot):
        return goes_up(slot) | goes_down(slot)

    def has_child(slot):
        across = (edge & (slot < 4)) | (fold & (z == 2) & (slot > 2))
        return across | (head & (slot == 3)) | ((slot == 2) & (((z == 2) & (outer != 3)) | ((z == 1) & ~fold & (outer != 0))))

    def deferred(slot):
        return (edge & (slot < 4)) | (fold & (z == 2) & (slot > 2))

    def order(place):
        last = jnp.where((z == 3) | chain, 1, 0)
        row = jnp.where(last == 1, jnp.where(chain, 1, 0), z)
        return digit(jnp.where(last == 1, TAKEN_LAST, TAKEN), row, place)

    def digit(table, row, place):
        digits = table // jnp.where(row == 0, 1, jnp.where(row == 1, 4**4, jnp.where(row == 2, 4**8, 4**12)))
        power = jnp.where(place == 0, 64, jnp.where(place == 1, 16, jnp.where(place == 2, 4, 1)))
        return (digits // power) % 4 + 1

    def back_order(place):
        return jnp.where(fold, digit(BACK_FOLD, (z + 2) % 4, place), order(3 - place))

    def half(side):
        return pl.ds(pl.multiple_of(side * TOK, TOK), TOK)

    def columns(first, count=DIM):
        return pl.ds(pl.multiple_of(first, DIM), count)

    local = []
    for r in range(GROUP):
        for n, (src, dst) in enumerate(((q_in, qbuf), (g_in, gbuf))):
            local.append(pltpu.make_async_copy(
                src.at[:, columns((core * GROUP + r) * DIM)], dst.at[r, half(core)], local_sem.at[n * GROUP + r]))
    for n, (src, dst) in enumerate(((k_in, kbuf), (v_in, vbuf))):
        local.append(pltpu.make_async_copy(
            src.at[:, columns(core * DIM)], dst.at[0, half(core)], local_sem.at[2 * GROUP + n]))
    for copy in local:
        copy.start()

    barrier = pltpu.get_barrier_semaphore()
    pl.semaphore_signal(barrier, 1, device_id=sibling, device_id_type=MESH)
    for d in range(1, 5):
        for is_there, other in ((d <= ahead, chip + d), (d <= behind, chip - d)):
            @pl.when(is_there)
            def _(other=other):
                for side in range(2):
                    pl.semaphore_signal(barrier, 1, device_id=device(other, side), device_id_type=MESH)
    met_count = 0
    for is_there, others in met:
        met_count += jnp.where(is_there, len(others), 0)

        @pl.when(is_there)
        def _(others=others):
            for other in others:
                pl.semaphore_signal(barrier, 1, device_id=device(*other), device_id_type=MESH)
    pl.semaphore_wait(barrier, 1 + 2 * (ahead + behind) + met_count)

    def remote(src, dst, send, recv, where):
        return pltpu.make_async_remote_copy(
            src_ref=src, dst_ref=dst, send_sem=send, recv_sem=recv, device_id=where, device_id_type=MESH)

    tensors = ((k_in, kbuf), (v_in, vbuf))

    def own_sends(t):
        src, buf = tensors[t]
        for n, d in enumerate((2, 1, 3, 4)):
            for side in range(2):
                yield sent(d), remote(
                    src.at[:, pl.ds(side * DIM, DIM)], buf.at[d, half(core)], kv_send.at[t, 2 * n + side],
                    kv_recv.at[t, d, core], device(chip + d, side))

    def own_hub_sends(t):
        src, buf = tensors[t]
        for side in range(2):
            yield edge, remote(
                src.at[:, pl.ds(side * DIM, DIM)], hub_ref.at[t, 0, half(core)], kv_send.at[t, 9 + side],
                hub_recv.at[t, 0, core], device(12, side))
        yield edge, remote(
            src.at[:, pl.ds(0, DIM)], buf.at[1, half(core)], kv_send.at[t, 11],
            kv_recv.at[t, 1, core], device(16, 0))
        yield edge, remote(
            src.at[:, pl.ds(DIM, DIM)], hub_ref.at[t, 1, half(core)], kv_send.at[t, 12],
            hub_recv.at[t, 1, core], device(3, 1))

    def hub_arrived(t, n, side):
        view = hub_ref.at[t, n, half(side)]
        return remote(view, view, kv_send.at[t, 8], hub_recv.at[t, n, side], sibling)

    def hub_sends(t, side):
        for k, (to, slot) in enumerate(((19, 4), (18, 3))):
            yield remote(hub_ref.at[t, 0, half(side)], tensors[t][1].at[slot, half(side)], hub_send.at[t, k, side],
                         kv_recv.at[t, slot, side], device(to, core))

    def round_send(t, slot, side):
        return remote(hub_ref.at[t, slot, half(side)], tensors[t][1].at[slot, half(side)], hub_send.at[t, slot - 1, side],
                      kv_recv.at[t, slot, side], device(16, core))

    def hub(t):
        @pl.when(chip == 12)
        def _():
            for side in range(2):
                hub_arrived(t, 0, side).wait_recv()
                for copy in hub_sends(t, side):
                    copy.start()

    def hub_round(t, slots):
        @pl.when((chip == 3) & (core == 1))
        def _():
            for slot in slots:
                for side in range(2):
                    hub_arrived(t, slot, side).wait_recv()
                    round_send(t, slot, side).start()

    def to_sibling(t):
        src, buf = tensors[t]
        return remote(src.at[:, columns((1 - core) * DIM)], buf.at[0, half(core)],
                      kv_send.at[t, 8], kv_recv.at[t, 0, core], sibling)

    def heads_to_sibling(n):
        src, dst = ((q_in, qbuf), (g_in, gbuf))[n]
        for r in range(GROUP):
            yield remote(src.at[:, columns(((1 - core) * GROUP + r) * DIM)], dst.at[r, half(core)],
                         qg_send.at[n, r], qg_recv.at[n, r], sibling)

    def start_if(cond, copy):
        @pl.when(cond)
        def _():
            copy.start()

    for cond, copy in list(own_hub_sends(0)) + list(own_sends(0)):
        start_if(cond, copy)
    to_sibling(0).start()
    for copy in heads_to_sibling(0):
        copy.start()
    to_sibling(1).start()
    for copy in heads_to_sibling(1):
        copy.start()

    position = chip * ROWS + lax.broadcasted_iota(jnp.int32, (1, ROWS), 1)

    def begins(n, first):
        edge = cu_ref[n]
        return jnp.where(edge <= position, edge, first)

    start_ref[...] = lax.fori_loop(0, cu_ref.shape[0], begins, jnp.zeros((1, ROWS), jnp.int32))
    m_ref[...] = jnp.full(m_ref.shape, HIDDEN, jnp.float32)
    l_ref[...] = jnp.zeros(l_ref.shape, jnp.float32)
    delta_ref[...] = jnp.zeros(delta_ref.shape, jnp.float32)
    dqt_ref[...] = jnp.zeros(dqt_ref.shape, jnp.float32)

    def arrived(t, slot, side):
        buf = tensors[t][1]
        view = buf.at[slot, half(side)]
        return remote(view, view, kv_send.at[t, 8], kv_recv.at[t, slot, side], sibling)

    def relay(t, slot, side):
        buf = tensors[t][1]
        down = goes_down(slot)
        to = jnp.where(down, slot - 1, slot + 1)
        return remote(buf.at[slot, half(side)], buf.at[to, half(side)], relay_send.at[t, slot, side],
                      kv_recv.at[t, to, side], device(jnp.where(down, chip - 1, chip + 1), core))

    def take(t, slot):
        @pl.when(there(slot))
        def _():
            for side in range(2):
                arrived(t, slot, side).wait_recv()
                wide = edge & (core == 1)
                start_if(handed_on(slot) & ~wide, relay(t, slot, side))

                @pl.when(handed_on(slot) & wide)
                def _():
                    remote(tensors[t][1].at[slot, half(side)], hub_ref.at[t, slot + 1, half(side)],
                           relay_send.at[t, slot, side], hub_recv.at[t, slot + 1, side], device(3, core)).start()

    def units(slot, body):
        @pl.when(there(slot))
        def _():
            def step(n, carry):
                body(slot, n // GROUP, n % GROUP, slot * 2 * GROUP + n)
                return carry
            lax.fori_loop(0, 2 * GROUP, step, 0, unroll=True)

    def scores(slot, side, r, unit, diagonal=False):
        s = dot(kbuf[slot, half(side)], qbuf[r], NT) * TO_LOG2
        first = (chip - slot) * ROWS + side * TOK
        row = lax.broadcasted_iota(jnp.int32, s.shape, 0)
        seen = row >= start_ref[...] - first
        if diagonal:
            seen &= row + side * TOK <= lax.broadcasted_iota(jnp.int32, s.shape, 1)
        s = jnp.where(seen, s, HIDDEN)
        old = m_ref[r]
        new = jnp.maximum(old, jnp.max(s, axis=0, keepdims=True))
        e = jnp.exp2(s - new)
        l_ref[r] = l_ref[r] * jnp.exp2(old - new) + jnp.sum(e, axis=0, keepdims=True)
        m_ref[r] = new
        mu_ref[unit] = new
        e_ref[unit] = e

    def share(unit, r):
        return jnp.exp2(mu_ref[unit] - m_ref[r]) * l_ref[r]

    def values(slot):
        @pl.when(there(slot))
        def _():
            for side in range(2):
                def step(r, acc):
                    unit = slot * 2 * GROUP + side * GROUP + r
                    p = e_ref[unit] * share(unit, r)
                    return acc + dot(p.astype(jnp.bfloat16), gbuf[r])
                part_ref[1, slot, pl.ds(side * TOK, TOK)] = lax.fori_loop(
                    0, GROUP, step, jnp.zeros((TOK, DIM), jnp.float32), unroll=True)

    def prob_grads(slot, side, r, unit):
        d = dot(vbuf[slot, half(side)], gbuf[r], NT)
        d_ref[unit] = d
        delta_ref[r] += jnp.sum(e_ref[unit] * d, axis=0, keepdims=True) * share(unit, r)

    def keys(slot):
        @pl.when(there(slot))
        def _():
            for side in range(2):
                def step(r, acc):
                    unit = slot * 2 * GROUP + side * GROUP + r
                    ds = (e_ref[unit] * share(unit, r) * (d_ref[unit] - delta_ref[r])).astype(jnp.bfloat16)
                    dqt_ref[r] += dot(kbuf[slot, pl.ds(side * TOK, TOK)], ds, TN)
                    return acc + dot(ds, qbuf[r])
                part_ref[0, slot, pl.ds(side * TOK, TOK)] = SCALE * lax.fori_loop(
                    0, GROUP, step, jnp.zeros((TOK, DIM), jnp.float32), unroll=True)

    def back_arrived(t, index, side):
        view = back_ref.at[t, index, half(side)]
        return remote(view, view, out_send.at[0], back_recv.at[t, index, side], sibling)

    def give(t, slot, side):
        over = fold & (slot > z)
        index = jnp.where(z == 0, slot + 3, jnp.where(
            z == 1, jnp.where(slot == 4, 7, slot + 5), jnp.where(z == 2, 10 - slot, 4)))
        index = jnp.where(over, index, slot - 1)
        to = jnp.where(z == 0, 15, jnp.where(z == 1, jnp.where(slot == 4, 16, 18), 0))
        to = jnp.where(over, to, chip - slot)
        down = (z == 3) & (slot == 3) & ~edge
        up = (z == 0) & (slot == 1) & ~fold
        index = jnp.where(down | up, 6, index)
        to = jnp.where(down, chip - 1, jnp.where(up, chip + 1, to))
        return remote(give_ref.at[t, slot, half(side)], back_ref.at[t, index, half(side)],
                      back_send.at[t, slot, side], back_recv.at[t, index, side], device(to, core))

    def send_back(t, slot):
        @pl.when(there(slot))
        def _():
            for side in range(2):
                rows = half(side)

                @pl.when(has_child(slot))
                def _():
                    back_arrived(t, slot + 4, side).wait_recv()
                    part_ref[t, slot, rows] += back_ref[t, slot + 4, rows].astype(jnp.float32)

                give_ref[t, slot, rows] = part_ref[t, slot, rows].astype(jnp.bfloat16)
                give(t, slot, side).start()

    def given(d):
        across = (z + d > 3) & (outer != 3) & (outer != 7)
        if d == 1:
            return (z < 3) | (across & (z < 3))
        if d == 3:
            return ((z == 0) & (outer == 3)) | across
        return (z + d <= 3) | across

    def hub_back_sends(t, side):
        rows = half(side)
        for k, src in enumerate((back_ref.at[t, 6, rows], give_ref.at[t, 1, rows])):
            yield remote(src, back_ref.at[t, 8, rows], hub_back_send.at[t, k, side],
                         back_recv.at[t, 8, side], device(14 + k, core))

    def hub_back(t):
        @pl.when(chip == 0)
        def _():
            for side in range(2):
                rows = half(side)
                _, summed = hub_back_sends(t, side)
                back_arrived(t, 4, side).wait_recv()
                back_arrived(t, 7, side).wait_recv()
                both = back_ref[t, 4, rows].astype(jnp.float32) + back_ref[t, 7, rows].astype(jnp.float32)
                give_ref[t, 1, rows] = both.astype(jnp.bfloat16)
                summed.start()
            for side in range(2):
                straight, _ = hub_back_sends(t, side)
                back_arrived(t, 6, side).wait_recv()
                straight.start()

    for n in list(range(GROUP)) + [2 * GROUP]:
        local[2 * n if n < GROUP else n].wait()
    arrived(0, 0, 1 - core).wait_recv()
    for copy in heads_to_sibling(0):
        copy.wait_recv()
    units(0, functools.partial(scores, diagonal=True))

    def key_step(place, carry):
        slot = order(place)

        @pl.when(place == 0)
        def _():
            hub(0)
            hub_round(0, (1, 2, 3, 4))

        take(0, slot)

        @pl.when(place == 0)
        def _():
            for cond, copy in list(own_hub_sends(1)) + list(own_sends(1)):
                start_if(cond, copy)

        @pl.when(place == 1)
        def _():
            hub_round(1, (1, 2))

        @pl.when(place == 3)
        def _():
            hub(1)
            hub_round(1, (3, 4))
            take(1, order(0))

        units(slot, scores)
        return carry

    lax.fori_loop(0, 4, key_step, 0)
    l_ref[...] = 1.0 / l_ref[...]

    for n in range(GROUP):
        local[2 * n + 1].wait()
    local[2 * GROUP + 1].wait()
    arrived(1, 0, 1 - core).wait_recv()
    for copy in heads_to_sibling(1):
        copy.wait_recv()

    units(0, prob_grads)

    def value_step(place, carry):
        slot = back_order(place)
        values(slot)

        @pl.when(~deferred(slot))
        def _():
            send_back(1, slot)

        units(order(place), prob_grads)

        @pl.when(place < 3)
        def _():
            take(1, order(place + 1))

        before = back_order(place - 2)

        @pl.when((place > 1) & deferred(before))
        def _():
            send_back(1, before)
        return carry

    lax.fori_loop(0, 4, value_step, 0)
    values(0)
    hub_back(1)

    def grad_step(place, carry):
        slot = back_order(place)
        keys(slot)
        early = back_order(place + 2)

        @pl.when((place < 2) & deferred(early))
        def _():
            send_back(1, early)

        before = back_order(place - 2)

        @pl.when((place > 1) & deferred(before))
        def _():
            send_back(0, before)

        @pl.when(~deferred(slot))
        def _():
            send_back(0, slot)
        return carry

    lax.fori_loop(0, 4, grad_step, 0)
    keys(0)
    hub_back(0)

    for r in range(GROUP):
        dq_ref[:, r * DIM:(r + 1) * DIM] = (jnp.transpose(dqt_ref[r]) * SCALE).astype(jnp.bfloat16)
    wide = columns(core * GROUP * DIM, GROUP * DIM)
    dq_far = remote(dq_ref.at[half(1 - core)], dq_out.at[:, wide], out_send.at[0], out_recv.at[0], sibling)
    dq_far.start()
    dq_near = pltpu.make_async_copy(dq_ref.at[half(core)], dq_out.at[:, wide], local_sem.at[0])
    dq_near.start()

    def late_step(place, carry):
        slot = back_order(place + 2)

        @pl.when(deferred(slot))
        def _():
            send_back(0, slot)
        return carry

    lax.fori_loop(0, 2, late_step, 0)

    copies = []
    for t, out in ((1, dv_out), (0, dk_out)):
        for is_there, index in [(given(d), d - 1) for d in range(1, 5)] + [(edge, 4), ((outer == 3) & (z > 1), 8)]:
            @pl.when(is_there)
            def _(index=index):
                for side in range(2):
                    back_arrived(t, index, side).wait_recv()
                part_ref[t, 0] += back_ref[t, index].astype(jnp.float32)
        give_ref[t, 0] = part_ref[t, 0].astype(jnp.bfloat16)
        narrow = columns(core * DIM)
        far = remote(give_ref.at[t, 0, half(1 - core)], out.at[:, narrow], out_send.at[1 + t], out_recv.at[1 + t], sibling)
        near = pltpu.make_async_copy(give_ref.at[t, 0, half(core)], out.at[:, narrow], local_sem.at[1 + t])
        far.start()
        near.start()
        copies += [far, near]

    for t in range(2):
        for cond, copy in own_sends(t):
            @pl.when(cond)
            def _(copy=copy):
                copy.wait_send()
        to_sibling(t).wait_send()
        for copy in heads_to_sibling(t):
            copy.wait_send()
        @pl.when(chip == 12)
        def _(t=t):
            for side in range(2):
                for copy in hub_sends(t, side):
                    copy.wait_send()

        for cond, copy in own_hub_sends(t):
            @pl.when(cond)
            def _(copy=copy):
                copy.wait_send()

        @pl.when((chip == 3) & (core == 1))
        def _(t=t):
            for slot in range(1, 5):
                for side in range(2):
                    round_send(t, slot, side).wait_send()

        @pl.when(chip == 0)
        def _(t=t):
            for side in range(2):
                for copy in hub_back_sends(t, side):
                    copy.wait_send()

        for slot in range(1, 5):
            @pl.when(handed_on(slot))
            def _(slot=slot):
                for side in range(2):
                    relay(t, slot, side).wait_send()

            @pl.when(there(slot))
            def _(slot=slot):
                for side in range(2):
                    give(t, slot, side).wait_send()
    for copy in [dq_far, dq_near] + copies:
        copy.wait()


def per_device(query_states, key_states, value_states, out_grad, cu_seqlens):
    f32, bf16, i32 = jnp.float32, jnp.bfloat16, jnp.int32
    vmem, dma = pltpu.VMEM, pltpu.SemaphoreType.DMA
    anywhere = pl.BlockSpec(memory_space=pl.ANY)
    return pl.pallas_call(
        kernel,
        out_shape=(
            jax.ShapeDtypeStruct(query_states.shape, bf16),
            jax.ShapeDtypeStruct(key_states.shape, bf16),
            jax.ShapeDtypeStruct(value_states.shape, bf16),
        ),
        in_specs=[pl.BlockSpec(memory_space=pltpu.SMEM)] + [anywhere] * 4,
        out_specs=(anywhere,) * 3,
        scratch_shapes=[
            vmem((GROUP, ROWS, DIM), bf16), vmem((GROUP, ROWS, DIM), bf16),
            vmem((5, ROWS, DIM), bf16), vmem((5, ROWS, DIM), bf16),
            vmem((10 * GROUP, TOK, ROWS), f32), vmem((10 * GROUP, TOK, ROWS), f32),
            vmem((10 * GROUP, 1, ROWS), f32), vmem((GROUP, 1, ROWS), f32),
            vmem((GROUP, 1, ROWS), f32), vmem((GROUP, 1, ROWS), f32), vmem((1, ROWS), i32),
            vmem((2, 5, ROWS, DIM), f32), vmem((2, 9, ROWS, DIM), bf16), vmem((2, 5, ROWS, DIM), bf16),
            vmem((GROUP, DIM, ROWS), f32), vmem((ROWS, GROUP * DIM), bf16),
            dma((2 * GROUP + 2,)), dma((2, GROUP)), dma((2, GROUP)), dma((2, 13)), dma((2, 5, 2)), dma((2, 5, 2)),
            dma((2, 5, 2)), dma((2, 9, 2)), dma((3,)), dma((3,)),
            vmem((2, 5, ROWS, DIM), bf16), dma((2, 5, 2)), dma((2, 4, 2)), dma((2, 2, 2)),
        ],
        compiler_params=pltpu.CompilerParams(
            collective_id=0, has_side_effects=True, vmem_limit_bytes=60 << 20),
        name="attention_grads",
    )(cu_seqlens, query_states, key_states, value_states, out_grad)


def solution(mesh):
    split = P(("dp", "outer", "inner"), None)
    return jax.shard_map(
        per_device,
        mesh=mesh,
        in_specs=(split, split, split, split, P("dp")),
        out_specs=(split, split, split),
        check_vma=False,
    )
```

```python
import functools

import jax
import jax.numpy as jnp
from jax import lax
from jax.experimental import pallas as pl
from jax.experimental.pallas import tpu as pltpu
from jax.sharding import PartitionSpec as P

GROUP = 4
DIM = 128
TOK = 256
ROWS = 2 * TOK
SCALE = DIM**-0.5
TO_LOG2 = SCALE * 1.4426950408889634
HIDDEN = -1e30
MESH = pl.DeviceIdType.MESH
NT = (((1,), (1,)), ((), ()))
TN = (((0,), (0,)), ((), ()))

def packed(orders):
    return sum(
        (distance - 1) * 4 ** (4 * row + 3 - place)
        for row, order in enumerate(orders)
        for place, distance in enumerate(order)
    )


TAKEN = packed(((4, 3, 2, 1), (2, 4, 1, 3), (2, 1, 4, 3)))
TAKEN_LAST = packed(((1, 2, 4, 3), (1, 2, 3, 4)))


def dot(a, b, dims=(((1,), (0,)), ((), ()))):
    return lax.dot_general(a, b, dims, preferred_element_type=jnp.float32)


def kernel(
    cu_ref, q_in, k_in, v_in, g_in,
    dq_out, dk_out, dv_out,
    qbuf, gbuf, kbuf, vbuf, e_ref, d_ref, mu_ref, m_ref, l_ref, delta_ref, start_ref,
    part_ref, back_ref, give_ref, dqt_ref, dq_ref,
    local_sem, qg_send, qg_recv, kv_send, kv_recv, relay_send, back_send, back_recv, out_send, out_recv,
    hub_ref, hub_recv, hub_send, hub_back_send,
):
    outer, inner = lax.axis_index("outer"), lax.axis_index("inner")
    core = inner % 2
    z = inner // 2
    chip = outer * 4 + z
    fold = outer == 4
    ahead, behind = jnp.minimum(4, 31 - chip), jnp.minimum(4, chip)
    edge = (outer == 3) & (z == 3)
    chain = edge | fold
    head = fold & (z == 0)
    met = (
        (chip == 12, ((18, core), (19, core))),
        (fold & (z > 1), ((12, core),)),
        (chip == 0, ((14, core), (15, core), (18, core), (19, core))),
        (((outer == 3) | fold) & (z > 1), ((0, core),)),
        (chip == 3, ((15, 0), (15, 1), (16, core))),
        (edge, ((3, 0), (3, 1))),
        (head, ((3, core),)),
    )

    def device(which, side):
        return {"outer": which // 4, "inner": (which % 4) * 2 + side}

    sibling = device(chip, 1 - core)

    def sent(d):
        if d == 1:
            return z < 3
        if d == 2:
            return ((z < 2) & ~fold) | edge | ((z > 1) & (outer != 3) & (outer != 7))
        within = (z + d <= 3) & ~fold
        if d == 3:
            within &= z > 0
        return within | ((z + d > 3) & (outer != 3) & (outer != 7))

    def there(slot):
        return (slot <= z) | (outer != 0)

    def goes_down(slot):
        return (z == 1) & (slot == 2) & ~fold & (outer != 0)

    def goes_up(slot):
        return (
            (edge & (slot < 4)) | (head & ((slot == 2) | (slot == 3)))
            | (fold & (z == 1) & ((slot == 1) | (slot == 3))) | (fold & (z == 2) & (slot < 3))
            | ((z == 2) & (slot == 2))
        )

    def handed_on(slot):
        return goes_up(slot) | goes_down(slot)

    joint = jnp.where(fold & (z == 1), 1, 2)
    has_joint = (z == 1) & (outer != 0) | (z == 2) & (outer != 3)

    def has_child(slot):
        return (head & (slot < 4)) | (has_joint & (slot == joint))

    def order(place):
        last = jnp.where((z == 3) | chain, 1, 0)
        row = jnp.where(last == 1, jnp.where(chain, 1, 0), z)
        return digit(jnp.where(last == 1, TAKEN_LAST, TAKEN), row, place)

    def digit(table, row, place):
        digits = table // jnp.where(row == 0, 1, jnp.where(row == 1, 4**4, jnp.where(row == 2, 4**8, 4**12)))
        power = jnp.where(place == 0, 64, jnp.where(place == 1, 16, jnp.where(place == 2, 4, 1)))
        return (digits // power) % 4 + 1

    def back_order(place):
        return jnp.where(fold & (z == 2), (place + 2) % 4 + 1, order(3 - place))

    def half(side):
        return pl.ds(pl.multiple_of(side * TOK, TOK), TOK)

    def columns(first, count=DIM):
        return pl.ds(pl.multiple_of(first, DIM), count)

    local = []
    for r in range(GROUP):
        for n, (src, dst) in enumerate(((q_in, qbuf), (g_in, gbuf))):
            local.append(pltpu.make_async_copy(
                src.at[:, columns((core * GROUP + r) * DIM)], dst.at[r, half(core)], local_sem.at[n * GROUP + r]))
    for n, (src, dst) in enumerate(((k_in, kbuf), (v_in, vbuf))):
        local.append(pltpu.make_async_copy(
            src.at[:, columns(core * DIM)], dst.at[0, half(core)], local_sem.at[2 * GROUP + n]))
    for copy in local:
        copy.start()

    barrier = pltpu.get_barrier_semaphore()
    pl.semaphore_signal(barrier, 1, device_id=sibling, device_id_type=MESH)
    for d in range(1, 5):
        for is_there, other in ((d <= ahead, chip + d), (d <= behind, chip - d)):
            @pl.when(is_there)
            def _(other=other):
                for side in range(2):
                    pl.semaphore_signal(barrier, 1, device_id=device(other, side), device_id_type=MESH)
    met_count = 0
    for is_there, others in met:
        met_count += jnp.where(is_there, len(others), 0)

        @pl.when(is_there)
        def _(others=others):
            for other in others:
                pl.semaphore_signal(barrier, 1, device_id=device(*other), device_id_type=MESH)
    pl.semaphore_wait(barrier, 1 + 2 * (ahead + behind) + met_count)

    def remote(src, dst, send, recv, where):
        return pltpu.make_async_remote_copy(
            src_ref=src, dst_ref=dst, send_sem=send, recv_sem=recv, device_id=where, device_id_type=MESH)

    tensors = ((k_in, kbuf), (v_in, vbuf))

    def own_sends(t):
        src, buf = tensors[t]
        for n, d in enumerate((2, 1, 3, 4)):
            for side in range(2):
                yield sent(d), remote(
                    src.at[:, pl.ds(side * DIM, DIM)], buf.at[d, half(core)], kv_send.at[t, 2 * n + side],
                    kv_recv.at[t, d, core], device(chip + d, side))

    def own_hub_sends(t):
        src, buf = tensors[t]
        for side in range(2):
            yield edge, remote(
                src.at[:, pl.ds(side * DIM, DIM)], hub_ref.at[t, 0, half(core)], kv_send.at[t, 9 + side],
                hub_recv.at[t, 0, core], device(12, side))
        yield edge, remote(
            src.at[:, pl.ds(0, DIM)], buf.at[1, half(core)], kv_send.at[t, 11],
            kv_recv.at[t, 1, core], device(16, 0))
        yield edge, remote(
            src.at[:, pl.ds(DIM, DIM)], hub_ref.at[t, 1, half(core)], kv_send.at[t, 12],
            hub_recv.at[t, 1, core], device(3, 1))

    def hub_arrived(t, n, side):
        view = hub_ref.at[t, n, half(side)]
        return remote(view, view, kv_send.at[t, 8], hub_recv.at[t, n, side], sibling)

    def hub_sends(t, side):
        for k, (to, slot) in enumerate(((19, 4), (18, 3))):
            yield remote(hub_ref.at[t, 0, half(side)], tensors[t][1].at[slot, half(side)], hub_send.at[t, k, side],
                         kv_recv.at[t, slot, side], device(to, core))

    def round_send(t, slot, side):
        return remote(hub_ref.at[t, slot, half(side)], tensors[t][1].at[slot, half(side)], hub_send.at[t, slot - 1, side],
                      kv_recv.at[t, slot, side], device(16, core))

    def hub(t):
        @pl.when(chip == 12)
        def _():
            for side in range(2):
                hub_arrived(t, 0, side).wait_recv()
                for copy in hub_sends(t, side):
                    copy.start()

    def hub_round(t, slots):
        @pl.when((chip == 3) & (core == 1))
        def _():
            for slot in slots:
                for side in range(2):
                    hub_arrived(t, slot, side).wait_recv()
                    round_send(t, slot, side).start()

    def to_sibling(t):
        src, buf = tensors[t]
        return remote(src.at[:, columns((1 - core) * DIM)], buf.at[0, half(core)],
                      kv_send.at[t, 8], kv_recv.at[t, 0, core], sibling)

    def heads_to_sibling(n):
        src, dst = ((q_in, qbuf), (g_in, gbuf))[n]
        for r in range(GROUP):
            yield remote(src.at[:, columns(((1 - core) * GROUP + r) * DIM)], dst.at[r, half(core)],
                         qg_send.at[n, r], qg_recv.at[n, r], sibling)

    def start_if(cond, copy):
        @pl.when(cond)
        def _():
            copy.start()

    for cond, copy in list(own_hub_sends(0)) + list(own_sends(0)):
        start_if(cond, copy)
    to_sibling(0).start()
    for copy in heads_to_sibling(0):
        copy.start()
    to_sibling(1).start()
    for copy in heads_to_sibling(1):
        copy.start()

    position = chip * ROWS + lax.broadcasted_iota(jnp.int32, (1, ROWS), 1)

    def begins(n, first):
        edge = cu_ref[n]
        return jnp.where(edge <= position, edge, first)

    start_ref[...] = lax.fori_loop(0, cu_ref.shape[0], begins, jnp.zeros((1, ROWS), jnp.int32))
    m_ref[...] = jnp.full(m_ref.shape, HIDDEN, jnp.float32)
    l_ref[...] = jnp.zeros(l_ref.shape, jnp.float32)
    delta_ref[...] = jnp.zeros(delta_ref.shape, jnp.float32)
    dqt_ref[...] = jnp.zeros(dqt_ref.shape, jnp.float32)

    def arrived(t, slot, side):
        buf = tensors[t][1]
        view = buf.at[slot, half(side)]
        return remote(view, view, kv_send.at[t, 8], kv_recv.at[t, slot, side], sibling)

    def relay(t, slot, side):
        buf = tensors[t][1]
        down = goes_down(slot)
        to = jnp.where(down, slot - 1, slot + 1)
        return remote(buf.at[slot, half(side)], buf.at[to, half(side)], relay_send.at[t, slot, side],
                      kv_recv.at[t, to, side], device(jnp.where(down, chip - 1, chip + 1), core))

    def take(t, slot):
        @pl.when(there(slot))
        def _():
            for side in range(2):
                arrived(t, slot, side).wait_recv()
                wide = edge & (core == 1)
                start_if(handed_on(slot) & ~wide, relay(t, slot, side))

                @pl.when(handed_on(slot) & wide)
                def _():
                    remote(tensors[t][1].at[slot, half(side)], hub_ref.at[t, slot + 1, half(side)],
                           relay_send.at[t, slot, side], hub_recv.at[t, slot + 1, side], device(3, core)).start()

    def units(slot, body):
        @pl.when(there(slot))
        def _():
            def step(n, carry):
                body(slot, n // GROUP, n % GROUP, slot * 2 * GROUP + n)
                return carry
            lax.fori_loop(0, 2 * GROUP, step, 0, unroll=True)

    def scores(slot, side, r, unit, diagonal=False):
        s = dot(kbuf[slot, half(side)], qbuf[r], NT) * TO_LOG2
        first = (chip - slot) * ROWS + side * TOK
        row = lax.broadcasted_iota(jnp.int32, s.shape, 0)
        seen = row >= start_ref[...] - first
        if diagonal:
            seen &= row + side * TOK <= lax.broadcasted_iota(jnp.int32, s.shape, 1)
        s = jnp.where(seen, s, HIDDEN)
        old = m_ref[r]
        new = jnp.maximum(old, jnp.max(s, axis=0, keepdims=True))
        e = jnp.exp2(s - new)
        l_ref[r] = l_ref[r] * jnp.exp2(old - new) + jnp.sum(e, axis=0, keepdims=True)
        m_ref[r] = new
        mu_ref[unit] = new
        e_ref[unit] = e

    def share(unit, r):
        return jnp.exp2(mu_ref[unit] - m_ref[r]) * l_ref[r]

    def values(slot):
        @pl.when(there(slot))
        def _():
            for side in range(2):
                def step(r, acc):
                    unit = slot * 2 * GROUP + side * GROUP + r
                    p = e_ref[unit] * share(unit, r)
                    return acc + dot(p.astype(jnp.bfloat16), gbuf[r])
                part_ref[1, slot, pl.ds(side * TOK, TOK)] = lax.fori_loop(
                    0, GROUP, step, jnp.zeros((TOK, DIM), jnp.float32), unroll=True)

    def prob_grads(slot, side, r, unit):
        d = dot(vbuf[slot, half(side)], gbuf[r], NT)
        d_ref[unit] = d
        delta_ref[r] += jnp.sum(e_ref[unit] * d, axis=0, keepdims=True) * share(unit, r)

    def keys(slot):
        @pl.when(there(slot))
        def _():
            for side in range(2):
                def step(r, acc):
                    unit = slot * 2 * GROUP + side * GROUP + r
                    ds = (e_ref[unit] * share(unit, r) * (d_ref[unit] - delta_ref[r])).astype(jnp.bfloat16)
                    dqt_ref[r] += dot(kbuf[slot, pl.ds(side * TOK, TOK)], ds, TN)
                    return acc + dot(ds, qbuf[r])
                part_ref[0, slot, pl.ds(side * TOK, TOK)] = SCALE * lax.fori_loop(
                    0, GROUP, step, jnp.zeros((TOK, DIM), jnp.float32), unroll=True)

    def back_arrived(t, index, side):
        view = back_ref.at[t, index, half(side)]
        return remote(view, view, out_send.at[0], back_recv.at[t, index, side], sibling)

    def give(t, slot, side):
        over = fold & (slot > z) & (z > 0)
        index = jnp.where(z == 1, slot + 3, jnp.where(z == 2, 10 - slot, 4))
        index = jnp.where(over, index, slot - 1)
        to = jnp.where(over, jnp.where(z == 1, 16, 0), chip - slot)
        merged = fold & (z == 2) & (slot == 2)
        index = jnp.where(merged, 5, index)
        to = jnp.where(merged, 17, to)
        down = (z == 3) & (slot == 3) & ~edge
        up = (z == 0) & (slot == 1) & ~fold
        index = jnp.where(down | up, 6, index)
        to = jnp.where(down, chip - 1, jnp.where(up, chip + 1, to))
        return remote(give_ref.at[t, slot, half(side)], back_ref.at[t, index, half(side)],
                      back_send.at[t, slot, side], back_recv.at[t, index, side], device(to, core))

    def send_back(t, slot):
        @pl.when(there(slot))
        def _():
            for side in range(2):
                rows = half(side)

                @pl.when(has_child(slot))
                def _():
                    back_arrived(t, slot + 4, side).wait_recv()
                    part_ref[t, slot, rows] += back_ref[t, slot + 4, rows].astype(jnp.float32)

                give_ref[t, slot, rows] = part_ref[t, slot, rows].astype(jnp.bfloat16)
                give(t, slot, side).start()

    def given(d):
        across = ((z + d > 3) & (outer != 3) & (outer != 7)) | ((outer == 3) & (z + d == 4))
        if d == 1:
            return (z < 3) | edge
        if d == 3:
            return ((z == 0) & (outer == 3)) | across
        return ((z + d <= 3) & ~head) | across

    def hub_back_sends(t, side):
        rows = half(side)
        for k, src in enumerate((back_ref.at[t, 6, rows], give_ref.at[t, 1, rows])):
            yield remote(src, back_ref.at[t, 8, rows], hub_back_send.at[t, k, side],
                         back_recv.at[t, 8, side], device(14 + k, core))

    def hub_back(t):
        @pl.when(chip == 0)
        def _():
            for side in range(2):
                rows = half(side)
                _, summed = hub_back_sends(t, side)
                back_arrived(t, 4, side).wait_recv()
                back_arrived(t, 7, side).wait_recv()
                both = back_ref[t, 4, rows].astype(jnp.float32) + back_ref[t, 7, rows].astype(jnp.float32)
                give_ref[t, 1, rows] = both.astype(jnp.bfloat16)
                summed.start()
            for side in range(2):
                straight, _ = hub_back_sends(t, side)
                back_arrived(t, 6, side).wait_recv()
                straight.start()

    for n in list(range(GROUP)) + [2 * GROUP]:
        local[2 * n if n < GROUP else n].wait()
    arrived(0, 0, 1 - core).wait_recv()
    for copy in heads_to_sibling(0):
        copy.wait_recv()
    units(0, functools.partial(scores, diagonal=True))

    def key_step(place, carry):
        slot = order(place)

        @pl.when(place == 0)
        def _():
            hub(0)
            hub_round(0, (1, 2, 3, 4))

        take(0, slot)

        @pl.when(place == 0)
        def _():
            for cond, copy in list(own_hub_sends(1)) + list(own_sends(1)):
                start_if(cond, copy)

        @pl.when(place == 1)
        def _():
            hub_round(1, (1, 2))

        @pl.when(place == 3)
        def _():
            hub(1)
            hub_round(1, (3, 4))

        early = jnp.where(chain, place - 1, place - 3)

        @pl.when((early >= 0) & ((early < 2) | edge))
        def _():
            take(1, order(early))

        units(slot, scores)
        return carry

    lax.fori_loop(0, 4, key_step, 0)
    l_ref[...] = 1.0 / l_ref[...]

    for n in range(GROUP):
        local[2 * n + 1].wait()
    local[2 * GROUP + 1].wait()
    arrived(1, 0, 1 - core).wait_recv()
    for copy in heads_to_sibling(1):
        copy.wait_recv()

    units(0, prob_grads)

    def value_step(place, carry):
        slot = back_order(place)
        values(slot)

        @pl.when(~has_child(slot))
        def _():
            send_back(1, slot)

        @pl.when(place == 1)
        def _():
            values(0)

        units(order(place), prob_grads)

        ahead_of = jnp.where(chain, 2, 1)

        @pl.when((place < 4 - ahead_of) & ~(edge & (place == 0)))
        def _():
            take(1, order(place + ahead_of))
        return carry

    lax.fori_loop(0, 4, value_step, 0)
    hub_back(1)

    def grad_step(place, carry):
        slot = back_order(place)
        keys(slot)

        @pl.when(~has_child(slot))
        def _():
            send_back(0, slot)

        waiting = jnp.where(head, 3 - place, joint)

        @pl.when((head & (place < 3)) | (has_joint & (place == 3)))
        def _():
            send_back(1, waiting)
        return carry

    lax.fori_loop(0, 4, grad_step, 0)
    keys(0)
    hub_back(0)

    @pl.when(head)
    def _():
        for slot in (3, 2, 1):
            send_back(0, slot)

    @pl.when(has_joint & ~fold)
    def _():
        send_back(0, joint)

    for r in range(GROUP):
        dq_ref[:, r * DIM:(r + 1) * DIM] = (jnp.transpose(dqt_ref[r]) * SCALE).astype(jnp.bfloat16)
    wide = columns(core * GROUP * DIM, GROUP * DIM)
    dq_far = remote(dq_ref.at[half(1 - core)], dq_out.at[:, wide], out_send.at[0], out_recv.at[0], sibling)
    dq_far.start()
    dq_near = pltpu.make_async_copy(dq_ref.at[half(core)], dq_out.at[:, wide], local_sem.at[0])
    dq_near.start()

    @pl.when(has_joint & fold)
    def _():
        send_back(0, joint)

    copies = []
    for t, out in ((1, dv_out), (0, dk_out)):
        for is_there, index in [(given(d), d - 1) for d in range(1, 5)] + [((outer == 3) & (z > 1), 8)]:
            @pl.when(is_there)
            def _(index=index):
                for side in range(2):
                    back_arrived(t, index, side).wait_recv()
                part_ref[t, 0] += back_ref[t, index].astype(jnp.float32)
        give_ref[t, 0] = part_ref[t, 0].astype(jnp.bfloat16)
        narrow = columns(core * DIM)
        far = remote(give_ref.at[t, 0, half(1 - core)], out.at[:, narrow], out_send.at[1 + t], out_recv.at[1 + t], sibling)
        near = pltpu.make_async_copy(give_ref.at[t, 0, half(core)], out.at[:, narrow], local_sem.at[1 + t])
        far.start()
        near.start()
        copies += [far, near]

    for t in range(2):
        for cond, copy in own_sends(t):
            @pl.when(cond)
            def _(copy=copy):
                copy.wait_send()
        to_sibling(t).wait_send()
        for copy in heads_to_sibling(t):
            copy.wait_send()
        @pl.when(chip == 12)
        def _(t=t):
            for side in range(2):
                for copy in hub_sends(t, side):
                    copy.wait_send()

        for cond, copy in own_hub_sends(t):
            @pl.when(cond)
            def _(copy=copy):
                copy.wait_send()

        @pl.when((chip == 3) & (core == 1))
        def _(t=t):
            for slot in range(1, 5):
                for side in range(2):
                    round_send(t, slot, side).wait_send()

        @pl.when(chip == 0)
        def _(t=t):
            for side in range(2):
                for copy in hub_back_sends(t, side):
                    copy.wait_send()

        for slot in range(1, 5):
            @pl.when(handed_on(slot))
            def _(slot=slot):
                for side in range(2):
                    relay(t, slot, side).wait_send()

            @pl.when(there(slot))
            def _(slot=slot):
                for side in range(2):
                    give(t, slot, side).wait_send()
    for copy in [dq_far, dq_near] + copies:
        copy.wait()


def per_device(query_states, key_states, value_states, out_grad, cu_seqlens):
    f32, bf16, i32 = jnp.float32, jnp.bfloat16, jnp.int32
    vmem, dma = pltpu.VMEM, pltpu.SemaphoreType.DMA
    anywhere = pl.BlockSpec(memory_space=pl.ANY)
    return pl.pallas_call(
        kernel,
        out_shape=(
            jax.ShapeDtypeStruct(query_states.shape, bf16),
            jax.ShapeDtypeStruct(key_states.shape, bf16),
            jax.ShapeDtypeStruct(value_states.shape, bf16),
        ),
        in_specs=[pl.BlockSpec(memory_space=pltpu.SMEM)] + [anywhere] * 4,
        out_specs=(anywhere,) * 3,
        scratch_shapes=[
            vmem((GROUP, ROWS, DIM), bf16), vmem((GROUP, ROWS, DIM), bf16),
            vmem((5, ROWS, DIM), bf16), vmem((5, ROWS, DIM), bf16),
            vmem((10 * GROUP, TOK, ROWS), f32), vmem((10 * GROUP, TOK, ROWS), f32),
            vmem((10 * GROUP, 1, ROWS), f32), vmem((GROUP, 1, ROWS), f32),
            vmem((GROUP, 1, ROWS), f32), vmem((GROUP, 1, ROWS), f32), vmem((1, ROWS), i32),
            vmem((2, 5, ROWS, DIM), f32), vmem((2, 9, ROWS, DIM), bf16), vmem((2, 5, ROWS, DIM), bf16),
            vmem((GROUP, DIM, ROWS), f32), vmem((ROWS, GROUP * DIM), bf16),
            dma((2 * GROUP + 2,)), dma((2, GROUP)), dma((2, GROUP)), dma((2, 13)), dma((2, 5, 2)), dma((2, 5, 2)),
            dma((2, 5, 2)), dma((2, 9, 2)), dma((3,)), dma((3,)),
            vmem((2, 5, ROWS, DIM), bf16), dma((2, 5, 2)), dma((2, 4, 2)), dma((2, 2, 2)),
        ],
        compiler_params=pltpu.CompilerParams(
            collective_id=0, has_side_effects=True, vmem_limit_bytes=60 << 20),
        name="attention_grads",
    )(cu_seqlens, query_states, key_states, value_states, out_grad)


def solution(mesh):
    split = P(("dp", "outer", "inner"), None)
    return jax.shard_map(
        per_device,
        mesh=mesh,
        in_specs=(split, split, split, split, P("dp")),
        out_specs=(split, split, split),
        check_vma=False,
    )
```

```python
import functools

import jax
import jax.numpy as jnp
from jax import lax
from jax.experimental import pallas as pl
from jax.experimental.pallas import tpu as pltpu
from jax.sharding import PartitionSpec as P

GROUP = 4
DIM = 128
TOK = 256
ROWS = 2 * TOK
SCALE = DIM**-0.5
TO_LOG2 = SCALE * 1.4426950408889634
HIDDEN = -1e30
MESH = pl.DeviceIdType.MESH
NT = (((1,), (1,)), ((), ()))
TN = (((0,), (0,)), ((), ()))

def packed(orders):
    return sum(
        (distance - 1) * 4 ** (4 * row + 3 - place)
        for row, order in enumerate(orders)
        for place, distance in enumerate(order)
    )


TAKEN = packed(((4, 3, 2, 1), (2, 4, 1, 3), (2, 1, 4, 3)))
TAKEN_LAST = packed(((1, 2, 4, 3), (1, 2, 3, 4)))


def dot(a, b, dims=(((1,), (0,)), ((), ()))):
    return lax.dot_general(a, b, dims, preferred_element_type=jnp.float32)


def kernel(
    cu_ref, q_in, k_in, v_in, g_in,
    dq_out, dk_out, dv_out,
    qbuf, gbuf, kbuf, vbuf, e_ref, d_ref, mu_ref, m_ref, l_ref, delta_ref, start_ref,
    part_ref, back_ref, give_ref, dqt_ref, dq_ref,
    local_sem, qg_send, qg_recv, kv_send, kv_recv, relay_send, back_send, back_recv, out_send, out_recv,
    hub_ref, hub_recv, hub_send, hub_back_send,
):
    outer, inner = lax.axis_index("outer"), lax.axis_index("inner")
    core = inner % 2
    z = inner // 2
    chip = outer * 4 + z
    fold = outer == 4
    ahead, behind = jnp.minimum(4, 31 - chip), jnp.minimum(4, chip)
    edge = (outer == 3) & (z == 3)
    chain = edge | fold
    head = fold & (z == 0)
    met = (
        (chip == 12, ((18, core), (19, core))),
        (fold & (z > 1), ((12, core),)),
        (chip == 0, ((14, core), (15, core), (18, core), (19, core))),
        (((outer == 3) | fold) & (z > 1), ((0, core),)),
        (chip == 3, ((15, 0), (15, 1), (16, core))),
        (edge, ((3, 0), (3, 1))),
        (head, ((3, core),)),
    )

    def device(which, side):
        return {"outer": which // 4, "inner": (which % 4) * 2 + side}

    sibling = device(chip, 1 - core)

    def sent(d):
        if d == 1:
            return z < 3
        if d == 2:
            return ((z < 2) & ~fold) | edge | ((z > 1) & (outer != 3) & (outer != 7))
        within = (z + d <= 3) & ~fold
        if d == 3:
            within &= z > 0
        return within | ((z + d > 3) & (outer != 3) & (outer != 7))

    def there(slot):
        return (slot <= z) | (outer != 0)

    def goes_down(slot):
        return (z == 1) & (slot == 2) & ~fold & (outer != 0)

    def goes_up(slot):
        return (
            (edge & (slot < 4)) | (head & ((slot == 2) | (slot == 3)))
            | (fold & (z == 1) & ((slot == 1) | (slot == 3))) | (fold & (z == 2) & (slot < 3))
            | ((z == 2) & (slot == 2))
        )

    def handed_on(slot):
        return goes_up(slot) | goes_down(slot)

    joint = jnp.where(fold & (z == 1), 1, 2)
    has_joint = (z == 1) & (outer != 0) | (z == 2) & (outer != 3)

    def has_child(slot):
        return (head & (slot < 4)) | (has_joint & (slot == joint))

    def order(place):
        last = jnp.where((z == 3) | chain, 1, 0)
        row = jnp.where(last == 1, jnp.where(chain, 1, 0), z)
        return digit(jnp.where(last == 1, TAKEN_LAST, TAKEN), row, place)

    def digit(table, row, place):
        digits = table // jnp.where(row == 0, 1, jnp.where(row == 1, 4**4, jnp.where(row == 2, 4**8, 4**12)))
        power = jnp.where(place == 0, 64, jnp.where(place == 1, 16, jnp.where(place == 2, 4, 1)))
        return (digits // power) % 4 + 1

    def back_order(place):
        return jnp.where(fold & (z == 2), (place + 2) % 4 + 1, order(3 - place))

    def half(side):
        return pl.ds(pl.multiple_of(side * TOK, TOK), TOK)

    def columns(first, count=DIM):
        return pl.ds(pl.multiple_of(first, DIM), count)

    local = []
    for r in range(GROUP):
        for n, (src, dst) in enumerate(((q_in, qbuf), (g_in, gbuf))):
            local.append(pltpu.make_async_copy(
                src.at[:, columns((core * GROUP + r) * DIM)], dst.at[r, half(core)], local_sem.at[n * GROUP + r]))
    for n, (src, dst) in enumerate(((k_in, kbuf), (v_in, vbuf))):
        local.append(pltpu.make_async_copy(
            src.at[:, columns(core * DIM)], dst.at[0, half(core)], local_sem.at[2 * GROUP + n]))
    for copy in local:
        copy.start()

    barrier = pltpu.get_barrier_semaphore()
    pl.semaphore_signal(barrier, 1, device_id=sibling, device_id_type=MESH)
    for d in range(1, 5):
        for is_there, other in ((d <= ahead, chip + d), (d <= behind, chip - d)):
            @pl.when(is_there)
            def _(other=other):
                for side in range(2):
                    pl.semaphore_signal(barrier, 1, device_id=device(other, side), device_id_type=MESH)
    met_count = 0
    for is_there, others in met:
        met_count += jnp.where(is_there, len(others), 0)

        @pl.when(is_there)
        def _(others=others):
            for other in others:
                pl.semaphore_signal(barrier, 1, device_id=device(*other), device_id_type=MESH)
    pl.semaphore_wait(barrier, 1 + 2 * (ahead + behind) + met_count)

    def remote(src, dst, send, recv, where):
        return pltpu.make_async_remote_copy(
            src_ref=src, dst_ref=dst, send_sem=send, recv_sem=recv, device_id=where, device_id_type=MESH)

    tensors = ((k_in, kbuf), (v_in, vbuf))

    def own_sends(t):
        src, buf = tensors[t]
        for n, d in enumerate((2, 1, 3, 4)):
            for side in range(2):
                yield sent(d), remote(
                    src.at[:, pl.ds(side * DIM, DIM)], buf.at[d, half(core)], kv_send.at[t, 2 * n + side],
                    kv_recv.at[t, d, core], device(chip + d, side))

    def own_hub_sends(t):
        src, buf = tensors[t]
        for side in range(2):
            yield edge, remote(
                src.at[:, pl.ds(side * DIM, DIM)], hub_ref.at[t, 0, half(core)], kv_send.at[t, 9 + side],
                hub_recv.at[t, 0, core], device(12, side))
        yield edge, remote(
            src.at[:, pl.ds(0, DIM)], buf.at[1, half(core)], kv_send.at[t, 11],
            kv_recv.at[t, 1, core], device(16, 0))
        yield edge, remote(
            src.at[:, pl.ds(DIM, DIM)], hub_ref.at[t, 1, half(core)], kv_send.at[t, 12],
            hub_recv.at[t, 1, core], device(3, 1))

    def hub_arrived(t, n, side):
        view = hub_ref.at[t, n, half(side)]
        return remote(view, view, kv_send.at[t, 8], hub_recv.at[t, n, side], sibling)

    def hub_sends(t, side):
        for k, (to, slot) in enumerate(((19, 4), (18, 3))):
            yield remote(hub_ref.at[t, 0, half(side)], tensors[t][1].at[slot, half(side)], hub_send.at[t, k, side],
                         kv_recv.at[t, slot, side], device(to, core))

    def round_send(t, slot, side):
        return remote(hub_ref.at[t, slot, half(side)], tensors[t][1].at[slot, half(side)], hub_send.at[t, slot - 1, side],
                      kv_recv.at[t, slot, side], device(16, core))

    def hub(t):
        @pl.when(chip == 12)
        def _():
            for side in range(2):
                hub_arrived(t, 0, side).wait_recv()
                for copy in hub_sends(t, side):
                    copy.start()

    def hub_round(t, slots):
        @pl.when((chip == 3) & (core == 1))
        def _():
            for slot in slots:
                for side in range(2):
                    hub_arrived(t, slot, side).wait_recv()
                    round_send(t, slot, side).start()

    def to_sibling(t):
        src, buf = tensors[t]
        return remote(src.at[:, columns((1 - core) * DIM)], buf.at[0, half(core)],
                      kv_send.at[t, 8], kv_recv.at[t, 0, core], sibling)

    def heads_to_sibling(n):
        src, dst = ((q_in, qbuf), (g_in, gbuf))[n]
        for r in range(GROUP):
            yield remote(src.at[:, columns(((1 - core) * GROUP + r) * DIM)], dst.at[r, half(core)],
                         qg_send.at[n, r], qg_recv.at[n, r], sibling)

    def start_if(cond, copy):
        @pl.when(cond)
        def _():
            copy.start()

    for cond, copy in list(own_hub_sends(0)) + list(own_sends(0)):
        start_if(cond, copy)
    to_sibling(0).start()
    for copy in heads_to_sibling(0):
        copy.start()
    to_sibling(1).start()
    for copy in heads_to_sibling(1):
        copy.start()

    position = chip * ROWS + lax.broadcasted_iota(jnp.int32, (1, ROWS), 1)

    def begins(n, first):
        edge = cu_ref[n]
        return jnp.where(edge <= position, edge, first)

    start_ref[...] = lax.fori_loop(0, cu_ref.shape[0], begins, jnp.zeros((1, ROWS), jnp.int32))
    m_ref[...] = jnp.full(m_ref.shape, HIDDEN, jnp.float32)
    l_ref[...] = jnp.zeros(l_ref.shape, jnp.float32)
    delta_ref[...] = jnp.zeros(delta_ref.shape, jnp.float32)
    dqt_ref[...] = jnp.zeros(dqt_ref.shape, jnp.float32)

    def arrived(t, slot, side):
        buf = tensors[t][1]
        view = buf.at[slot, half(side)]
        return remote(view, view, kv_send.at[t, 8], kv_recv.at[t, slot, side], sibling)

    def relay(t, slot, side):
        buf = tensors[t][1]
        down = goes_down(slot)
        to = jnp.where(down, slot - 1, slot + 1)
        return remote(buf.at[slot, half(side)], buf.at[to, half(side)], relay_send.at[t, slot, side],
                      kv_recv.at[t, to, side], device(jnp.where(down, chip - 1, chip + 1), core))

    def take(t, slot):
        @pl.when(there(slot))
        def _():
            for side in range(2):
                arrived(t, slot, side).wait_recv()
                wide = edge & (core == 1)
                start_if(handed_on(slot) & ~wide, relay(t, slot, side))

                @pl.when(handed_on(slot) & wide)
                def _():
                    remote(tensors[t][1].at[slot, half(side)], hub_ref.at[t, slot + 1, half(side)],
                           relay_send.at[t, slot, side], hub_recv.at[t, slot + 1, side], device(3, core)).start()

    def units(slot, body):
        @pl.when(there(slot))
        def _():
            def step(n, carry):
                body(slot, n // GROUP, n % GROUP, slot * 2 * GROUP + n)
                return carry
            lax.fori_loop(0, 2 * GROUP, step, 0, unroll=True)

    def scores(slot, side, r, unit, diagonal=False):
        s = dot(kbuf[slot, half(side)], qbuf[r], NT) * TO_LOG2
        first = (chip - slot) * ROWS + side * TOK
        row = lax.broadcasted_iota(jnp.int32, s.shape, 0)
        seen = row >= start_ref[...] - first
        if diagonal:
            seen &= row + side * TOK <= lax.broadcasted_iota(jnp.int32, s.shape, 1)
        s = jnp.where(seen, s, HIDDEN)
        old = m_ref[r]
        new = jnp.maximum(old, jnp.max(s, axis=0, keepdims=True))
        e = jnp.exp2(s - new)
        l_ref[r] = l_ref[r] * jnp.exp2(old - new) + jnp.sum(e, axis=0, keepdims=True)
        m_ref[r] = new
        mu_ref[unit] = new
        e_ref[unit] = e

    def share(unit, r):
        return jnp.exp2(mu_ref[unit] - m_ref[r]) * l_ref[r]

    def values(slot):
        @pl.when(there(slot))
        def _():
            for side in range(2):
                def step(r, acc):
                    unit = slot * 2 * GROUP + side * GROUP + r
                    p = e_ref[unit] * share(unit, r)
                    return acc + dot(p.astype(jnp.bfloat16), gbuf[r])
                part_ref[1, slot, pl.ds(side * TOK, TOK)] = lax.fori_loop(
                    0, GROUP, step, jnp.zeros((TOK, DIM), jnp.float32), unroll=True)

    def prob_grads(slot, side, r, unit):
        d = dot(vbuf[slot, half(side)], gbuf[r], NT)
        d_ref[unit] = d
        delta_ref[r] += jnp.sum(e_ref[unit] * d, axis=0, keepdims=True) * share(unit, r)

    def keys(slot):
        @pl.when(there(slot))
        def _():
            for side in range(2):
                def step(r, acc):
                    unit = slot * 2 * GROUP + side * GROUP + r
                    ds = (e_ref[unit] * share(unit, r) * (d_ref[unit] - delta_ref[r])).astype(jnp.bfloat16)
                    dqt_ref[r] += dot(kbuf[slot, pl.ds(side * TOK, TOK)], ds, TN)
                    return acc + dot(ds, qbuf[r])
                part_ref[0, slot, pl.ds(side * TOK, TOK)] = SCALE * lax.fori_loop(
                    0, GROUP, step, jnp.zeros((TOK, DIM), jnp.float32), unroll=True)
                send_half(0, slot, side)

    def send_half(t, slot, side):
        if not isinstance(slot, int):
            @pl.when(~has_child(slot))
            def _():
                rows = half(side)
                give_ref[t, slot, rows] = part_ref[t, slot, rows].astype(jnp.bfloat16)
                give(t, slot, side).start()

    def back_arrived(t, index, side):
        view = back_ref.at[t, index, half(side)]
        return remote(view, view, out_send.at[0], back_recv.at[t, index, side], sibling)

    def give(t, slot, side):
        over = fold & (slot > z) & (z > 0)
        index = jnp.where(z == 1, slot + 3, jnp.where(z == 2, 10 - slot, 4))
        index = jnp.where(over, index, slot - 1)
        to = jnp.where(over, jnp.where(z == 1, 16, 0), chip - slot)
        merged = fold & (z == 2) & (slot == 2)
        index = jnp.where(merged, 5, index)
        to = jnp.where(merged, 17, to)
        down = (z == 3) & (slot == 3) & ~edge
        up = (z == 0) & (slot == 1) & ~fold
        index = jnp.where(down | up, 6, index)
        to = jnp.where(down, chip - 1, jnp.where(up, chip + 1, to))
        return remote(give_ref.at[t, slot, half(side)], back_ref.at[t, index, half(side)],
                      back_send.at[t, slot, side], back_recv.at[t, index, side], device(to, core))

    def send_back(t, slot):
        @pl.when(there(slot))
        def _():
            for side in range(2):
                rows = half(side)

                @pl.when(has_child(slot))
                def _():
                    back_arrived(t, slot + 4, side).wait_recv()
                    part_ref[t, slot, rows] += back_ref[t, slot + 4, rows].astype(jnp.float32)

                give_ref[t, slot, rows] = part_ref[t, slot, rows].astype(jnp.bfloat16)
                give(t, slot, side).start()

    def given(d):
        across = ((z + d > 3) & (outer != 3) & (outer != 7)) | ((outer == 3) & (z + d == 4))
        if d == 1:
            return (z < 3) | edge
        if d == 3:
            return ((z == 0) & (outer == 3)) | across
        return ((z + d <= 3) & ~head) | across

    def hub_back_sends(t, side):
        rows = half(side)
        for k, src in enumerate((back_ref.at[t, 6, rows], give_ref.at[t, 1, rows])):
            yield remote(src, back_ref.at[t, 8, rows], hub_back_send.at[t, k, side],
                         back_recv.at[t, 8, side], device(14 + k, core))

    def hub_back(t):
        @pl.when(chip == 0)
        def _():
            for side in range(2):
                rows = half(side)
                _, summed = hub_back_sends(t, side)
                back_arrived(t, 4, side).wait_recv()
                back_arrived(t, 7, side).wait_recv()
                both = back_ref[t, 4, rows].astype(jnp.float32) + back_ref[t, 7, rows].astype(jnp.float32)
                give_ref[t, 1, rows] = both.astype(jnp.bfloat16)
                summed.start()
            for side in range(2):
                straight, _ = hub_back_sends(t, side)
                back_arrived(t, 6, side).wait_recv()
                straight.start()

    for n in list(range(GROUP)) + [2 * GROUP]:
        local[2 * n if n < GROUP else n].wait()
    arrived(0, 0, 1 - core).wait_recv()
    for copy in heads_to_sibling(0):
        copy.wait_recv()
    units(0, functools.partial(scores, diagonal=True))

    def key_step(place, carry):
        slot = order(place)

        @pl.when(place == 0)
        def _():
            hub(0)
            hub_round(0, (1, 2, 3, 4))

        take(0, slot)

        @pl.when(place == 0)
        def _():
            for cond, copy in list(own_hub_sends(1)) + list(own_sends(1)):
                start_if(cond, copy)

        @pl.when(place == 1)
        def _():
            hub_round(1, (1, 2))

        @pl.when(place == 3)
        def _():
            hub(1)
            hub_round(1, (3, 4))

        early = jnp.where(chain, place - 1, place - 3)

        @pl.when((early >= 0) & ((early < 2) | edge))
        def _():
            take(1, order(early))

        units(slot, scores)
        return carry

    lax.fori_loop(0, 4, key_step, 0)
    l_ref[...] = 1.0 / l_ref[...]

    for n in range(GROUP):
        local[2 * n + 1].wait()
    local[2 * GROUP + 1].wait()
    arrived(1, 0, 1 - core).wait_recv()
    for copy in heads_to_sibling(1):
        copy.wait_recv()

    units(0, prob_grads)

    def value_step(place, carry):
        slot = back_order(place)
        values(slot)

        @pl.when(~has_child(slot))
        def _():
            send_back(1, slot)

        @pl.when(place == 1)
        def _():
            values(0)

        units(order(place), prob_grads)

        ahead_of = jnp.where(chain, 2, 1)

        @pl.when((place < 4 - ahead_of) & ~(edge & (place == 0)))
        def _():
            take(1, order(place + ahead_of))
        return carry

    lax.fori_loop(0, 4, value_step, 0)
    hub_back(1)

    def grad_step(place, carry):
        slot = back_order(place)
        keys(slot)
        waiting = jnp.where(head, 3 - place, joint)

        @pl.when((head & (place < 3)) | (has_joint & (place == 3)))
        def _():
            send_back(1, waiting)
        return carry

    lax.fori_loop(0, 4, grad_step, 0)
    keys(0)
    hub_back(0)

    @pl.when(head)
    def _():
        for slot in (3, 2, 1):
            send_back(0, slot)

    @pl.when(has_joint & ~fold)
    def _():
        send_back(0, joint)

    for r in range(GROUP):
        dq_ref[:, r * DIM:(r + 1) * DIM] = (jnp.transpose(dqt_ref[r]) * SCALE).astype(jnp.bfloat16)
    wide = columns(core * GROUP * DIM, GROUP * DIM)
    dq_far = remote(dq_ref.at[half(1 - core)], dq_out.at[:, wide], out_send.at[0], out_recv.at[0], sibling)
    dq_far.start()
    dq_near = pltpu.make_async_copy(dq_ref.at[half(core)], dq_out.at[:, wide], local_sem.at[0])
    dq_near.start()

    @pl.when(has_joint & fold)
    def _():
        send_back(0, joint)

    copies = []
    for t, out in ((1, dv_out), (0, dk_out)):
        for is_there, index in [(given(d), d - 1) for d in range(1, 5)] + [((outer == 3) & (z > 1), 8)]:
            @pl.when(is_there)
            def _(index=index):
                for side in range(2):
                    back_arrived(t, index, side).wait_recv()
                part_ref[t, 0] += back_ref[t, index].astype(jnp.float32)
        give_ref[t, 0] = part_ref[t, 0].astype(jnp.bfloat16)
        narrow = columns(core * DIM)
        far = remote(give_ref.at[t, 0, half(1 - core)], out.at[:, narrow], out_send.at[1 + t], out_recv.at[1 + t], sibling)
        near = pltpu.make_async_copy(give_ref.at[t, 0, half(core)], out.at[:, narrow], local_sem.at[1 + t])
        far.start()
        near.start()
        copies += [far, near]

    for t in range(2):
        for cond, copy in own_sends(t):
            @pl.when(cond)
            def _(copy=copy):
                copy.wait_send()
        to_sibling(t).wait_send()
        for copy in heads_to_sibling(t):
            copy.wait_send()
        @pl.when(chip == 12)
        def _(t=t):
            for side in range(2):
                for copy in hub_sends(t, side):
                    copy.wait_send()

        for cond, copy in own_hub_sends(t):
            @pl.when(cond)
            def _(copy=copy):
                copy.wait_send()

        @pl.when((chip == 3) & (core == 1))
        def _(t=t):
            for slot in range(1, 5):
                for side in range(2):
                    round_send(t, slot, side).wait_send()

        @pl.when(chip == 0)
        def _(t=t):
            for side in range(2):
                for copy in hub_back_sends(t, side):
                    copy.wait_send()

        for slot in range(1, 5):
            @pl.when(handed_on(slot))
            def _(slot=slot):
                for side in range(2):
                    relay(t, slot, side).wait_send()

            @pl.when(there(slot))
            def _(slot=slot):
                for side in range(2):
                    give(t, slot, side).wait_send()
    for copy in [dq_far, dq_near] + copies:
        copy.wait()


def write_out(dq_in, dk_in, dv_in, dq_out, dk_out, dv_out):
    dq_out[...] = dq_in[...]
    dk_out[...] = dk_in[...]
    dv_out[...] = dv_in[...]


def per_device(query_states, key_states, value_states, out_grad, cu_seqlens):
    f32, bf16, i32 = jnp.float32, jnp.bfloat16, jnp.int32
    vmem, dma = pltpu.VMEM, pltpu.SemaphoreType.DMA
    anywhere = pl.BlockSpec(memory_space=pl.ANY)
    shapes = (
        jax.ShapeDtypeStruct(query_states.shape, bf16),
        jax.ShapeDtypeStruct(key_states.shape, bf16),
        jax.ShapeDtypeStruct(value_states.shape, bf16),
    )
    grads = pl.pallas_call(
        kernel,
        out_shape=shapes,
        in_specs=[pl.BlockSpec(memory_space=pltpu.SMEM)] + [anywhere] * 4,
        out_specs=(anywhere,) * 3,
        scratch_shapes=[
            vmem((GROUP, ROWS, DIM), bf16), vmem((GROUP, ROWS, DIM), bf16),
            vmem((5, ROWS, DIM), bf16), vmem((5, ROWS, DIM), bf16),
            vmem((10 * GROUP, TOK, ROWS), f32), vmem((10 * GROUP, TOK, ROWS), f32),
            vmem((10 * GROUP, 1, ROWS), f32), vmem((GROUP, 1, ROWS), f32),
            vmem((GROUP, 1, ROWS), f32), vmem((GROUP, 1, ROWS), f32), vmem((1, ROWS), i32),
            vmem((2, 5, ROWS, DIM), f32), vmem((2, 9, ROWS, DIM), bf16), vmem((2, 5, ROWS, DIM), bf16),
            vmem((GROUP, DIM, ROWS), f32), vmem((ROWS, GROUP * DIM), bf16),
            dma((2 * GROUP + 2,)), dma((2, GROUP)), dma((2, GROUP)), dma((2, 13)), dma((2, 5, 2)), dma((2, 5, 2)),
            dma((2, 5, 2)), dma((2, 9, 2)), dma((3,)), dma((3,)),
            vmem((2, 5, ROWS, DIM), bf16), dma((2, 5, 2)), dma((2, 4, 2)), dma((2, 2, 2)),
        ],
        compiler_params=pltpu.CompilerParams(
            collective_id=0, has_side_effects=True, vmem_limit_bytes=60 << 20),
        name="attention_grads",
    )(cu_seqlens, query_states, key_states, value_states, out_grad)
    rows = query_states.shape[0] // 2
    specs = tuple(pl.BlockSpec((rows, shape.shape[1]), lambda i: (i, 0)) for shape in shapes)
    return pl.pallas_call(
        write_out, grid=(2,), out_shape=shapes, in_specs=list(specs), out_specs=specs, name="write_out",
    )(*grads)


def solution(mesh):
    split = P(("dp", "outer", "inner"), None)
    return jax.shard_map(
        per_device,
        mesh=mesh,
        in_specs=(split, split, split, split, P("dp")),
        out_specs=(split, split, split),
        check_vma=False,
    )
```

```python
import functools

import jax
import jax.numpy as jnp
from jax import lax
from jax.experimental import pallas as pl
from jax.experimental.pallas import tpu as pltpu
from jax.sharding import PartitionSpec as P

GROUP = 4
DIM = 128
TOK = 256
ROWS = 2 * TOK
SCALE = DIM**-0.5
TO_LOG2 = SCALE * 1.4426950408889634
HIDDEN = -1e30
MESH = pl.DeviceIdType.MESH
NT = (((1,), (1,)), ((), ()))
TN = (((0,), (0,)), ((), ()))

def packed(orders):
    return sum(
        (distance - 1) * 4 ** (4 * row + 3 - place)
        for row, order in enumerate(orders)
        for place, distance in enumerate(order)
    )


TAKEN = packed(((4, 3, 2, 1), (2, 4, 1, 3), (2, 1, 4, 3)))
TAKEN_LAST = packed(((1, 2, 4, 3), (1, 2, 3, 4)))


def dot(a, b, dims=(((1,), (0,)), ((), ()))):
    return lax.dot_general(a, b, dims, preferred_element_type=jnp.float32)


def kernel(
    cu_ref, q_in, k_in, v_in, g_in,
    dq_out, dk_out, dv_out,
    qbuf, gbuf, kbuf, vbuf, e_ref, d_ref, mu_ref, m_ref, l_ref, delta_ref, start_ref,
    part_ref, back_ref, give_ref, dqt_ref, dq_ref,
    local_sem, qg_send, qg_recv, kv_send, kv_recv, relay_send, back_send, back_recv, out_send, out_recv,
    hub_ref, hub_recv, hub_send, hub_back_send,
):
    outer, inner = lax.axis_index("outer"), lax.axis_index("inner")
    core = inner % 2
    z = inner // 2
    chip = outer * 4 + z
    fold = outer == 4
    ahead, behind = jnp.minimum(4, 31 - chip), jnp.minimum(4, chip)
    edge = (outer == 3) & (z == 3)
    chain = edge | fold
    head = fold & (z == 0)
    met = (
        (chip == 12, ((18, core), (19, core))),
        (fold & (z > 1), ((12, core),)),
        (chip == 0, ((14, core), (15, core), (18, core), (19, core))),
        (((outer == 3) | fold) & (z > 1), ((0, core),)),
        (chip == 3, ((15, 0), (15, 1), (16, core))),
        (edge, ((3, 0), (3, 1))),
        (head, ((3, core),)),
    )

    def device(which, side):
        return {"outer": which // 4, "inner": (which % 4) * 2 + side}

    sibling = device(chip, 1 - core)

    def sent(d):
        if d == 1:
            return z < 3
        if d == 2:
            return ((z < 2) & ~fold) | edge | ((z > 1) & (outer != 3) & (outer != 7))
        within = (z + d <= 3) & ~fold
        if d == 3:
            within &= z > 0
        return within | ((z + d > 3) & (outer != 3) & (outer != 7))

    def there(slot):
        return (slot <= z) | (outer != 0)

    def goes_down(slot):
        return (z == 1) & (slot == 2) & ~fold & (outer != 0)

    def goes_up(slot):
        return (
            (edge & (slot < 4)) | (head & ((slot == 2) | (slot == 3)))
            | (fold & (z == 1) & ((slot == 1) | (slot == 3))) | (fold & (z == 2) & (slot < 3))
            | ((z == 2) & (slot == 2))
        )

    def handed_on(slot):
        return goes_up(slot) | goes_down(slot)

    joint = jnp.where(fold & (z == 1), 1, 2)
    has_joint = (z == 1) & (outer != 0) | (z == 2) & (outer != 3)

    def has_child(slot):
        return (head & (slot < 4)) | (has_joint & (slot == joint))

    def order(place):
        last = jnp.where((z == 3) | chain, 1, 0)
        row = jnp.where(last == 1, jnp.where(chain, 1, 0), z)
        return digit(jnp.where(last == 1, TAKEN_LAST, TAKEN), row, place)

    def digit(table, row, place):
        digits = table // jnp.where(row == 0, 1, jnp.where(row == 1, 4**4, jnp.where(row == 2, 4**8, 4**12)))
        power = jnp.where(place == 0, 64, jnp.where(place == 1, 16, jnp.where(place == 2, 4, 1)))
        return (digits // power) % 4 + 1

    def back_order(place):
        return jnp.where(fold & (z == 2), (place + 2) % 4 + 1, order(3 - place))

    def half(side):
        return pl.ds(pl.multiple_of(side * TOK, TOK), TOK)

    def columns(first, count=DIM):
        return pl.ds(pl.multiple_of(first, DIM), count)

    local = []
    for r in range(GROUP):
        for n, (src, dst) in enumerate(((q_in, qbuf), (g_in, gbuf))):
            local.append(pltpu.make_async_copy(
                src.at[:, columns((core * GROUP + r) * DIM)], dst.at[r, half(core)], local_sem.at[n * GROUP + r]))
    for n, (src, dst) in enumerate(((k_in, kbuf), (v_in, vbuf))):
        local.append(pltpu.make_async_copy(
            src.at[:, columns(core * DIM)], dst.at[0, half(core)], local_sem.at[2 * GROUP + n]))
    for copy in local:
        copy.start()

    barrier = pltpu.get_barrier_semaphore()
    pl.semaphore_signal(barrier, 1, device_id=sibling, device_id_type=MESH)
    for d in range(1, 5):
        for is_there, other in ((d <= ahead, chip + d), (d <= behind, chip - d)):
            @pl.when(is_there)
            def _(other=other):
                for side in range(2):
                    pl.semaphore_signal(barrier, 1, device_id=device(other, side), device_id_type=MESH)
    met_count = 0
    for is_there, others in met:
        met_count += jnp.where(is_there, len(others), 0)

        @pl.when(is_there)
        def _(others=others):
            for other in others:
                pl.semaphore_signal(barrier, 1, device_id=device(*other), device_id_type=MESH)
    pl.semaphore_wait(barrier, 1 + 2 * (ahead + behind) + met_count)

    def remote(src, dst, send, recv, where):
        return pltpu.make_async_remote_copy(
            src_ref=src, dst_ref=dst, send_sem=send, recv_sem=recv, device_id=where, device_id_type=MESH)

    tensors = ((k_in, kbuf), (v_in, vbuf))

    def own_sends(t):
        src, buf = tensors[t]
        for n, d in enumerate((2, 1, 3, 4)):
            for side in range(2):
                yield sent(d), remote(
                    src.at[:, pl.ds(side * DIM, DIM)], buf.at[d, half(core)], kv_send.at[t, 2 * n + side],
                    kv_recv.at[t, d, core], device(chip + d, side))

    def own_hub_sends(t):
        src, buf = tensors[t]
        for side in range(2):
            yield edge, remote(
                src.at[:, pl.ds(side * DIM, DIM)], hub_ref.at[t, 0, half(core)], kv_send.at[t, 9 + side],
                hub_recv.at[t, 0, core], device(12, side))
        yield edge, remote(
            src.at[:, pl.ds(0, DIM)], buf.at[1, half(core)], kv_send.at[t, 11],
            kv_recv.at[t, 1, core], device(16, 0))
        yield edge, remote(
            src.at[:, pl.ds(DIM, DIM)], hub_ref.at[t, 1, half(core)], kv_send.at[t, 12],
            hub_recv.at[t, 1, core], device(3, 1))

    def hub_arrived(t, n, side):
        view = hub_ref.at[t, n, half(side)]
        return remote(view, view, kv_send.at[t, 8], hub_recv.at[t, n, side], sibling)

    def hub_sends(t, side):
        for k, (to, slot) in enumerate(((19, 4), (18, 3))):
            yield remote(hub_ref.at[t, 0, half(side)], tensors[t][1].at[slot, half(side)], hub_send.at[t, k, side],
                         kv_recv.at[t, slot, side], device(to, core))

    def round_send(t, slot, side):
        return remote(hub_ref.at[t, slot, half(side)], tensors[t][1].at[slot, half(side)], hub_send.at[t, slot - 1, side],
                      kv_recv.at[t, slot, side], device(16, core))

    def hub(t):
        @pl.when(chip == 12)
        def _():
            for side in range(2):
                hub_arrived(t, 0, side).wait_recv()
                for copy in hub_sends(t, side):
                    copy.start()

    def hub_round(t, slots):
        @pl.when((chip == 3) & (core == 1))
        def _():
            for slot in slots:
                for side in range(2):
                    hub_arrived(t, slot, side).wait_recv()
                    round_send(t, slot, side).start()

    def to_sibling(t):
        src, buf = tensors[t]
        return remote(src.at[:, columns((1 - core) * DIM)], buf.at[0, half(core)],
                      kv_send.at[t, 8], kv_recv.at[t, 0, core], sibling)

    def heads_to_sibling(n):
        src, dst = ((q_in, qbuf), (g_in, gbuf))[n]
        for r in range(GROUP):
            yield remote(src.at[:, columns(((1 - core) * GROUP + r) * DIM)], dst.at[r, half(core)],
                         qg_send.at[n, r], qg_recv.at[n, r], sibling)

    def start_if(cond, copy):
        @pl.when(cond)
        def _():
            copy.start()

    for cond, copy in list(own_hub_sends(0)) + list(own_sends(0)):
        start_if(cond, copy)
    to_sibling(0).start()
    for copy in heads_to_sibling(0):
        copy.start()
    to_sibling(1).start()
    for copy in heads_to_sibling(1):
        copy.start()

    position = chip * ROWS + lax.broadcasted_iota(jnp.int32, (1, ROWS), 1)

    def begins(n, first):
        edge = cu_ref[n]
        return jnp.where(edge <= position, edge, first)

    start_ref[...] = lax.fori_loop(0, cu_ref.shape[0], begins, jnp.zeros((1, ROWS), jnp.int32))
    m_ref[...] = jnp.full(m_ref.shape, HIDDEN, jnp.float32)
    l_ref[...] = jnp.zeros(l_ref.shape, jnp.float32)
    delta_ref[...] = jnp.zeros(delta_ref.shape, jnp.float32)
    dqt_ref[...] = jnp.zeros(dqt_ref.shape, jnp.float32)

    def arrived(t, slot, side):
        buf = tensors[t][1]
        view = buf.at[slot, half(side)]
        return remote(view, view, kv_send.at[t, 8], kv_recv.at[t, slot, side], sibling)

    def relay(t, slot, side):
        buf = tensors[t][1]
        down = goes_down(slot)
        to = jnp.where(down, slot - 1, slot + 1)
        return remote(buf.at[slot, half(side)], buf.at[to, half(side)], relay_send.at[t, slot, side],
                      kv_recv.at[t, to, side], device(jnp.where(down, chip - 1, chip + 1), core))

    def take(t, slot):
        @pl.when(there(slot))
        def _():
            for side in range(2):
                arrived(t, slot, side).wait_recv()
                wide = edge & (core == 1)
                start_if(handed_on(slot) & ~wide, relay(t, slot, side))

                @pl.when(handed_on(slot) & wide)
                def _():
                    remote(tensors[t][1].at[slot, half(side)], hub_ref.at[t, slot + 1, half(side)],
                           relay_send.at[t, slot, side], hub_recv.at[t, slot + 1, side], device(3, core)).start()

    def units(slot, body):
        @pl.when(there(slot))
        def _():
            def step(n, carry):
                body(slot, n // GROUP, n % GROUP, slot * 2 * GROUP + n)
                return carry
            lax.fori_loop(0, 2 * GROUP, step, 0, unroll=True)

    def scores(slot, side, r, unit, diagonal=False):
        s = dot(kbuf[slot, half(side)], qbuf[r], NT) * TO_LOG2
        first = (chip - slot) * ROWS + side * TOK
        row = lax.broadcasted_iota(jnp.int32, s.shape, 0)
        seen = row >= start_ref[...] - first
        if diagonal:
            seen &= row + side * TOK <= lax.broadcasted_iota(jnp.int32, s.shape, 1)
        s = jnp.where(seen, s, HIDDEN)
        old = m_ref[r]
        new = jnp.maximum(old, jnp.max(s, axis=0, keepdims=True))
        e = jnp.exp2(s - new)
        l_ref[r] = l_ref[r] * jnp.exp2(old - new) + jnp.sum(e, axis=0, keepdims=True)
        m_ref[r] = new
        mu_ref[unit] = new
        e_ref[unit] = e

    def share(unit, r):
        return jnp.exp2(mu_ref[unit] - m_ref[r]) * l_ref[r]

    def values(slot):
        @pl.when(there(slot))
        def _():
            for side in range(2):
                def step(r, acc):
                    unit = slot * 2 * GROUP + side * GROUP + r
                    p = e_ref[unit] * share(unit, r)
                    return acc + dot(p.astype(jnp.bfloat16), gbuf[r])
                part_ref[1, slot, pl.ds(side * TOK, TOK)] = lax.fori_loop(
                    0, GROUP, step, jnp.zeros((TOK, DIM), jnp.float32), unroll=True)

    def prob_grads(slot, side, r, unit):
        d = dot(vbuf[slot, half(side)], gbuf[r], NT)
        d_ref[unit] = d
        delta_ref[r] += jnp.sum(e_ref[unit] * d, axis=0, keepdims=True) * share(unit, r)

    def keys(slot):
        @pl.when(there(slot))
        def _():
            for side in range(2):
                def step(r, acc):
                    unit = slot * 2 * GROUP + side * GROUP + r
                    ds = (e_ref[unit] * share(unit, r) * (d_ref[unit] - delta_ref[r])).astype(jnp.bfloat16)
                    dqt_ref[r] += dot(kbuf[slot, pl.ds(side * TOK, TOK)], ds, TN)
                    return acc + dot(ds, qbuf[r])
                part_ref[0, slot, pl.ds(side * TOK, TOK)] = SCALE * lax.fori_loop(
                    0, GROUP, step, jnp.zeros((TOK, DIM), jnp.float32), unroll=True)
                send_half(0, slot, side)

    def send_half(t, slot, side):
        if not isinstance(slot, int):
            @pl.when(~has_child(slot))
            def _():
                rows = half(side)
                give_ref[t, slot, rows] = part_ref[t, slot, rows].astype(jnp.bfloat16)
                give(t, slot, side).start()

    def back_arrived(t, index, side):
        view = back_ref.at[t, index, half(side)]
        return remote(view, view, out_send.at[0], back_recv.at[t, index, side], sibling)

    def give(t, slot, side):
        over = fold & (slot > z) & (z > 0)
        index = jnp.where(z == 1, slot + 3, jnp.where(z == 2, 10 - slot, 4))
        index = jnp.where(over, index, slot - 1)
        to = jnp.where(over, jnp.where(z == 1, 16, 0), chip - slot)
        merged = fold & (z == 2) & (slot == 2)
        index = jnp.where(merged, 5, index)
        to = jnp.where(merged, 17, to)
        down = (z == 3) & (slot == 3) & ~edge
        up = (z == 0) & (slot == 1) & ~fold
        index = jnp.where(down | up, 6, index)
        to = jnp.where(down, chip - 1, jnp.where(up, chip + 1, to))
        return remote(give_ref.at[t, slot, half(side)], back_ref.at[t, index, half(side)],
                      back_send.at[t, slot, side], back_recv.at[t, index, side], device(to, core))

    def send_back(t, slot):
        @pl.when(there(slot))
        def _():
            for side in range(2):
                rows = half(side)

                @pl.when(has_child(slot))
                def _():
                    back_arrived(t, slot + 4, side).wait_recv()
                    part_ref[t, slot, rows] += back_ref[t, slot + 4, rows].astype(jnp.float32)

                give_ref[t, slot, rows] = part_ref[t, slot, rows].astype(jnp.bfloat16)
                give(t, slot, side).start()

    def given(d):
        across = ((z + d > 3) & (outer != 3) & (outer != 7)) | ((outer == 3) & (z + d == 4))
        if d == 1:
            return (z < 3) | edge
        if d == 3:
            return ((z == 0) & (outer == 3)) | across
        return ((z + d <= 3) & ~head) | across

    def hub_back_sends(t, side):
        rows = half(side)
        for k, src in enumerate((back_ref.at[t, 6, rows], give_ref.at[t, 1, rows])):
            yield remote(src, back_ref.at[t, 8, rows], hub_back_send.at[t, k, side],
                         back_recv.at[t, 8, side], device(14 + k, core))

    def hub_back(t):
        @pl.when(chip == 0)
        def _():
            for side in range(2):
                rows = half(side)
                _, summed = hub_back_sends(t, side)
                back_arrived(t, 4, side).wait_recv()
                back_arrived(t, 7, side).wait_recv()
                both = back_ref[t, 4, rows].astype(jnp.float32) + back_ref[t, 7, rows].astype(jnp.float32)
                give_ref[t, 1, rows] = both.astype(jnp.bfloat16)
                summed.start()
            for side in range(2):
                straight, _ = hub_back_sends(t, side)
                back_arrived(t, 6, side).wait_recv()
                straight.start()

    for n in list(range(GROUP)) + [2 * GROUP]:
        local[2 * n if n < GROUP else n].wait()
    arrived(0, 0, 1 - core).wait_recv()
    for copy in heads_to_sibling(0):
        copy.wait_recv()
    units(0, functools.partial(scores, diagonal=True))

    def key_step(place, carry):
        slot = order(place)

        @pl.when(place == 0)
        def _():
            hub(0)
            hub_round(0, (1, 2, 3, 4))

        take(0, slot)

        @pl.when(place == 0)
        def _():
            for cond, copy in list(own_hub_sends(1)) + list(own_sends(1)):
                start_if(cond, copy)

        @pl.when(place == 1)
        def _():
            hub_round(1, (1, 2))

        @pl.when(place == 3)
        def _():
            hub(1)
            hub_round(1, (3, 4))

        early = jnp.where(chain, place - 1, place - 3)

        @pl.when((early >= 0) & ((early < 2) | edge))
        def _():
            take(1, order(early))

        units(slot, scores)
        return carry

    lax.fori_loop(0, 4, key_step, 0)
    l_ref[...] = 1.0 / l_ref[...]

    for n in range(GROUP):
        local[2 * n + 1].wait()
    local[2 * GROUP + 1].wait()
    arrived(1, 0, 1 - core).wait_recv()
    for copy in heads_to_sibling(1):
        copy.wait_recv()

    units(0, prob_grads)

    def value_step(place, carry):
        slot = back_order(place)
        values(slot)

        @pl.when(~has_child(slot))
        def _():
            send_back(1, slot)

        @pl.when(place == 1)
        def _():
            values(0)

        units(order(place), prob_grads)

        ahead_of = jnp.where(chain, 2, 1)

        @pl.when((place < 4 - ahead_of) & ~(edge & (place == 0)))
        def _():
            take(1, order(place + ahead_of))
        return carry

    lax.fori_loop(0, 4, value_step, 0)
    hub_back(1)

    def grad_step(place, carry):
        slot = back_order(place)
        keys(slot)
        waiting = jnp.where(head, 3 - place, joint)

        @pl.when((head & (place < 3)) | (has_joint & (place == 3)))
        def _():
            send_back(1, waiting)
        return carry

    lax.fori_loop(0, 4, grad_step, 0)

    @pl.when(head)
    def _():
        send_back(0, 3)

    keys(0)
    hub_back(0)

    @pl.when(head)
    def _():
        for slot in (2, 1):
            send_back(0, slot)

    @pl.when(has_joint & ~fold)
    def _():
        send_back(0, joint)

    for r in range(GROUP):
        dq_ref[:, r * DIM:(r + 1) * DIM] = (jnp.transpose(dqt_ref[r]) * SCALE).astype(jnp.bfloat16)
    wide = columns(core * GROUP * DIM, GROUP * DIM)
    dq_far = remote(dq_ref.at[half(1 - core)], dq_out.at[:, wide], out_send.at[0], out_recv.at[0], sibling)
    dq_far.start()
    dq_near = pltpu.make_async_copy(dq_ref.at[half(core)], dq_out.at[:, wide], local_sem.at[0])
    dq_near.start()

    @pl.when(has_joint & fold)
    def _():
        send_back(0, joint)

    copies = []
    for t, out in ((1, dv_out), (0, dk_out)):
        for is_there, index in [(given(d), d - 1) for d in range(1, 5)] + [((outer == 3) & (z > 1), 8)]:
            @pl.when(is_there)
            def _(index=index):
                for side in range(2):
                    back_arrived(t, index, side).wait_recv()
                part_ref[t, 0] += back_ref[t, index].astype(jnp.float32)
        give_ref[t, 0] = part_ref[t, 0].astype(jnp.bfloat16)
        narrow = columns(core * DIM)
        far = remote(give_ref.at[t, 0, half(1 - core)], out.at[:, narrow], out_send.at[1 + t], out_recv.at[1 + t], sibling)
        near = pltpu.make_async_copy(give_ref.at[t, 0, half(core)], out.at[:, narrow], local_sem.at[1 + t])
        far.start()
        near.start()
        copies += [far, near]

    for t in range(2):
        for cond, copy in own_sends(t):
            @pl.when(cond)
            def _(copy=copy):
                copy.wait_send()
        to_sibling(t).wait_send()
        for copy in heads_to_sibling(t):
            copy.wait_send()
        @pl.when(chip == 12)
        def _(t=t):
            for side in range(2):
                for copy in hub_sends(t, side):
                    copy.wait_send()

        for cond, copy in own_hub_sends(t):
            @pl.when(cond)
            def _(copy=copy):
                copy.wait_send()

        @pl.when((chip == 3) & (core == 1))
        def _(t=t):
            for slot in range(1, 5):
                for side in range(2):
                    round_send(t, slot, side).wait_send()

        @pl.when(chip == 0)
        def _(t=t):
            for side in range(2):
                for copy in hub_back_sends(t, side):
                    copy.wait_send()

        for slot in range(1, 5):
            @pl.when(handed_on(slot))
            def _(slot=slot):
                for side in range(2):
                    relay(t, slot, side).wait_send()

            @pl.when(there(slot))
            def _(slot=slot):
                for side in range(2):
                    give(t, slot, side).wait_send()
    for copy in [dq_far, dq_near] + copies:
        copy.wait()


def write_out(dq_in, dk_in, dv_in, dq_out, dk_out, dv_out):
    dq_out[...] = dq_in[...]
    dk_out[...] = dk_in[...]
    dv_out[...] = dv_in[...]


def per_device(query_states, key_states, value_states, out_grad, cu_seqlens):
    f32, bf16, i32 = jnp.float32, jnp.bfloat16, jnp.int32
    vmem, dma = pltpu.VMEM, pltpu.SemaphoreType.DMA
    anywhere = pl.BlockSpec(memory_space=pl.ANY)
    shapes = (
        jax.ShapeDtypeStruct(query_states.shape, bf16),
        jax.ShapeDtypeStruct(key_states.shape, bf16),
        jax.ShapeDtypeStruct(value_states.shape, bf16),
    )
    grads = pl.pallas_call(
        kernel,
        out_shape=shapes,
        in_specs=[pl.BlockSpec(memory_space=pltpu.SMEM)] + [anywhere] * 4,
        out_specs=(anywhere,) * 3,
        scratch_shapes=[
            vmem((GROUP, ROWS, DIM), bf16), vmem((GROUP, ROWS, DIM), bf16),
            vmem((5, ROWS, DIM), bf16), vmem((5, ROWS, DIM), bf16),
            vmem((10 * GROUP, TOK, ROWS), f32), vmem((10 * GROUP, TOK, ROWS), f32),
            vmem((10 * GROUP, 1, ROWS), f32), vmem((GROUP, 1, ROWS), f32),
            vmem((GROUP, 1, ROWS), f32), vmem((GROUP, 1, ROWS), f32), vmem((1, ROWS), i32),
            vmem((2, 5, ROWS, DIM), f32), vmem((2, 9, ROWS, DIM), bf16), vmem((2, 5, ROWS, DIM), bf16),
            vmem((GROUP, DIM, ROWS), f32), vmem((ROWS, GROUP * DIM), bf16),
            dma((2 * GROUP + 2,)), dma((2, GROUP)), dma((2, GROUP)), dma((2, 13)), dma((2, 5, 2)), dma((2, 5, 2)),
            dma((2, 5, 2)), dma((2, 9, 2)), dma((3,)), dma((3,)),
            vmem((2, 5, ROWS, DIM), bf16), dma((2, 5, 2)), dma((2, 4, 2)), dma((2, 2, 2)),
        ],
        compiler_params=pltpu.CompilerParams(
            collective_id=0, has_side_effects=True, vmem_limit_bytes=60 << 20),
        name="attention_grads",
    )(cu_seqlens, query_states, key_states, value_states, out_grad)
    rows = query_states.shape[0] // 2
    specs = tuple(pl.BlockSpec((rows, shape.shape[1]), lambda i: (i, 0)) for shape in shapes)
    return pl.pallas_call(
        write_out, grid=(2,), out_shape=shapes, in_specs=list(specs), out_specs=specs, name="write_out",
    )(*grads)


def solution(mesh):
    split = P(("dp", "outer", "inner"), None)
    return jax.shard_map(
        per_device,
        mesh=mesh,
        in_specs=(split, split, split, split, P("dp")),
        out_specs=(split, split, split),
        check_vma=False,
    )
```
